128 devices in a mesh: group: 8 (over x_hi, y), member: 16 (over z, x_lo, core).
Axes of the slice: x: 4 (x_hi: 2, x_lo: 2; x = x_hi * 2 + x_lo), y: 4, z: 4, core: 2. Of those that a mesh axis runs over, the one named last changes fastest.
Arguments:
- tokens: bfloat16 [16384, 2560], P(('group', 'member')), may hold values from -6 to 6
- route_ids: int32 [16384, 6], P(('group', 'member')), may hold values from 0 to 159, as said below
- route_gates: bfloat16 [16384, 6], P(('group', 'member')), may hold values from 0.099609375 to 1
- out_grad: bfloat16 [16384, 2560], P(('group', 'member')), may hold values from -6 to 6
- proj_in: float32 [2, 16, 2560, 384], P(None, 'member', 'group'), may hold values from -0.125 to 0.125
- proj_out: float32 [16, 2560, 384], P('member', 'group'), may hold values from -0.15625 to 0.15625
- first_moment: float32 [3, 16, 2560, 384], P(None, 'member', 'group'), may hold values from -12 to 12
- second_moment: float32 [3, 16, 2560, 384], P(None, 'member', 'group'), may hold values from 1 to 100
Outputs:
- layer_out: bfloat16 [16384, 2560], P(('group', 'member'))
- token_grad: bfloat16 [16384, 2560], P(('group', 'member'))
- new_proj_in: float32 [2, 16, 2560, 384], P(None, 'member', 'group')
- new_proj_out: float32 [16, 2560, 384], P('member', 'group')
- new_first: float32 [3, 16, 2560, 384], P(None, 'member', 'group')
- new_second: float32 [3, 16, 2560, 384], P(None, 'member', 'group')
The draws below stay inside these ranges and needn't reach their ends.
Inputs may be any that keep to these rules, and one draw needn't show every extreme that they name: `route_ids`: each row names 6 different experts. Ids below 4 are the window's experts; among the rows of one device each window expert is named by at most 80 rows, and in every group one window expert is named by exactly 80 rows of each device of the group.
All inputs are finite; a program needn't handle non-finite values.
Results may differ from the reference program's by a relative error of at most 0.023.
Values may be sent and summed in bfloat16 or wider, within the bound.
A program may use at most 128 MiB of HBM per device.

```python
import math
import jax
import jax.numpy as jnp
from jax import lax

D = 2560
FF = 1536
EXPERTS = 160
TOPK = 6
SPLIT = 4
TOK_DEV = 128
EXP_WIN = 4
PIECES = 16
FF_PIECE = 384
CAP = 80
TOKENS = 16384
N_GROUP = 8
N_MEMBER = 16


def draw_route_ids(key, part):
    key = jax.random.fold_in(key, 7)
    blocks = TOKENS // TOK_DEV
    members = EXP_WIN * SPLIT
    groups = blocks // members
    key_list = jax.random.split(key, 6)
    hot_group = jax.random.randint(key_list[0], (groups,), 0, EXP_WIN)
    hot_block = jnp.repeat(hot_group, members)
    expert_axis = jnp.arange(EXP_WIN, dtype=jnp.int32)
    counts = jax.random.randint(key_list[1], (blocks, EXP_WIN), CAP // 8, CAP // 2 + 1)
    counts = jnp.where(expert_axis[None, :] == hot_block[:, None], CAP, counts)
    shifts = jax.random.randint(key_list[2], (blocks, 1, 1), 0, TOK_DEV)
    spacing = TOK_DEV // EXP_WIN
    row_axis = jnp.arange(TOK_DEV, dtype=jnp.int32)
    offset = (row_axis[None, :, None] - shifts - expert_axis[None, None, :] * spacing) % TOK_DEV
    covered = offset < counts[:, None, :]
    ordinal = jnp.cumsum(covered.astype(jnp.int32), axis=2) - 1
    slot_axis = jnp.arange(TOPK, dtype=jnp.int32)
    chosen = covered[..., None] & (ordinal[..., None] == slot_axis)
    window_ids = jnp.sum(jnp.where(chosen, expert_axis[:, None], 0), axis=2)
    filled = jnp.sum(covered.astype(jnp.int32), axis=2, keepdims=True)
    start_other = jax.random.randint(key_list[3], (blocks, TOK_DEV, 1), 0, EXPERTS - EXP_WIN)
    others = EXP_WIN + (start_other + slot_axis) % (EXPERTS - EXP_WIN)
    route_table = jnp.where(slot_axis < filled, window_ids, others)
    slot_scores = jax.random.randint(key_list[4], (blocks, TOK_DEV, TOPK), 0, 4096) * TOPK + slot_axis
    slot_order = jnp.argsort(slot_scores, axis=2)
    route_table = jnp.take_along_axis(route_table, slot_order, axis=2)
    row_scores = jax.random.randint(key_list[5], (blocks, TOK_DEV), 0, 4096) * TOK_DEV + row_axis
    row_order = jnp.argsort(row_scores, axis=1)
    route_table = jnp.take_along_axis(route_table, row_order[:, :, None], axis=1)
    return route_table.reshape(TOKENS, TOPK).astype(jnp.int32)


def level_of(stream_key, shape, cuts, smallest, largest):
    factor_of = 1.0
    for dim, shards_of in cuts:
        draws = jax.random.uniform(jax.random.fold_in(jax.random.fold_in(stream_key, 6), dim), (shards_of,), jnp.float32, smallest / len(cuts), largest / len(cuts))
        factor_of = factor_of * jnp.repeat(jnp.exp(draws), shape[dim] // shards_of).reshape((-1,) + (1,) * (len(shape) - 1 - dim))
    return factor_of


def scatter_about(stream_key, shape, width, most, shards=(), held_as=jnp.bfloat16):
    array = width * jax.random.normal(stream_key, shape, jnp.float32)
    if shards:
        array = array * level_of(stream_key, shape, shards, -0.22, 0.18)
    return jnp.clip(array, -most, most).astype(held_as)


def setup_inputs(seed: int = 0) -> dict:
    streams_of = jax.random.split(jax.random.key(seed), 9)
    return {
        "tokens": scatter_about(streams_of[0], (TOKENS, D), 1.0, 6.0, ((0, 128),)),
        "route_ids": draw_route_ids(jax.random.fold_in(streams_of[8], 71), 0),
        "route_gates": jnp.clip(0.099609375 + 0.9003906 * jax.random.uniform(streams_of[2], (TOKENS, TOPK), jnp.float32) ** level_of(streams_of[2], (TOKENS, TOPK), ((0, 128),), -0.2, 0.2), 0.099609375, 1.0).astype(jnp.bfloat16),
        "out_grad": scatter_about(streams_of[3], (TOKENS, D), 1.0, 6.0, ((0, 128),)),
        "proj_in": scatter_about(streams_of[4], (2, PIECES, D, FF_PIECE), D ** -0.5, 0.125, ((1, 16), (2, 8)), jnp.float32),
        "proj_out": scatter_about(streams_of[5], (PIECES, D, FF_PIECE), FF ** -0.5, 0.15625, ((0, 16), (1, 8)), jnp.float32),
        "first_moment": scatter_about(streams_of[6], (3, PIECES, D, FF_PIECE), 2.0, 12.0, ((1, 16), (2, 8)), jnp.float32),
        "second_moment": jnp.clip(jnp.exp(math.log(100.0) - 4.6051702 * jax.random.uniform(streams_of[7], (3, PIECES, D, FF_PIECE), jnp.float32) ** level_of(streams_of[7], (3, PIECES, D, FF_PIECE), ((1, 16), (2, 8)), -0.2, 0.2)), 1.0, 100.0),
    }


beta_one = 0.9
beta_two = 0.95
learn_rate = 0.0003
decay_rate = 0.1
adam_eps = 1e-08
bias_one = 1.0 - 0.9 ** 10
bias_two = 1.0 - 0.95 ** 10

def route_tables(route_ids, route_gates):
    experts = jnp.arange(EXP_WIN, dtype=jnp.int32)
    hit_table = route_ids[:, :, None] == experts[None, None, :]
    matched = jnp.any(hit_table, axis=1)
    weights = lax.optimization_barrier(jnp.sum(jnp.where(hit_table, route_gates[:, :, None].astype(jnp.float32), jnp.float32(0.0)), axis=1))
    position = jnp.cumsum(matched.astype(jnp.int32), axis=0) - 1
    return (matched, weights, position)

def slot_selector(matched, position):
    slot_axis = jnp.arange(CAP, dtype=jnp.int32)
    return matched.T[:, None, :] & (position.T[:, None, :] == slot_axis[None, :, None])

def dispatch_rows(values, selector):
    moved = jnp.einsum('ect,td->ecd', selector.astype(jnp.float32), values.astype(jnp.float32))
    return moved.astype(jnp.bfloat16)

def slot_gates(weights, selector):
    return lax.optimization_barrier(jnp.sum(jnp.where(selector, weights.T[:, None, :], jnp.float32(0.0)), axis=2))

def collect_rows(pieces, matched, position):
    row_index = jnp.arange(EXP_WIN, dtype=jnp.int32)[None, :] * CAP + jnp.clip(position, 0, CAP - 1).astype(jnp.int32)
    gathered = jnp.take(pieces.reshape(EXP_WIN * CAP, -1), row_index, axis=0)
    return lax.optimization_barrier(jnp.sum(jnp.where(matched[:, :, None], gathered, jnp.float32(0.0)), axis=1))

def piece_work(row_block, gate_col, grad_block, w_gate, w_up, w_down):
    pre_gate = jnp.dot(row_block, w_gate, preferred_element_type=jnp.float32)
    pre_up = jnp.dot(row_block, w_up, preferred_element_type=jnp.float32)
    sigmoid_g = jax.nn.sigmoid(pre_gate)
    active = pre_gate * sigmoid_g
    hidden = (active * pre_up).astype(jnp.bfloat16)
    product = jnp.dot(hidden, w_down.T, preferred_element_type=jnp.float32)
    partial_value = (gate_col * product).astype(jnp.bfloat16)
    scaled = (gate_col * grad_block.astype(jnp.float32)).astype(jnp.bfloat16)
    d_hidden = jnp.dot(scaled, w_down, preferred_element_type=jnp.float32)
    d_active = sigmoid_g * (1.0 + pre_gate * (1.0 - sigmoid_g))
    d_gate = (d_hidden * pre_up * d_active).astype(jnp.bfloat16)
    d_up = (d_hidden * active).astype(jnp.bfloat16)
    input_part = (jnp.dot(d_gate, w_gate.T, preferred_element_type=jnp.float32) + jnp.dot(d_up, w_up.T, preferred_element_type=jnp.float32)).astype(jnp.bfloat16)
    grad_gate = jnp.dot(row_block.T, d_gate, preferred_element_type=jnp.float32)
    grad_up = jnp.dot(row_block.T, d_up, preferred_element_type=jnp.float32)
    grad_down = jnp.dot(scaled.T, hidden, preferred_element_type=jnp.float32)
    return (partial_value, input_part, jnp.stack([grad_gate, grad_up, grad_down]).astype(jnp.bfloat16))

def reference(tokens, route_ids, route_gates, out_grad, proj_in, proj_out, first_moment, second_moment):
    masters = jnp.concatenate([proj_in, proj_out[None]], axis=0)
    weights_bf = masters.astype(jnp.bfloat16)
    grouped = (tokens.reshape(N_GROUP, N_MEMBER, TOK_DEV, D), route_ids.reshape(N_GROUP, N_MEMBER, TOK_DEV, TOPK), route_gates.reshape(N_GROUP, N_MEMBER, TOK_DEV, TOPK), out_grad.reshape(N_GROUP, N_MEMBER, TOK_DEV, D))

    def group_step(grad_sum, group_in):
        token_block, id_block, gate_block, cot_block = group_in
        matched, weights, position = jax.vmap(route_tables)(id_block, gate_block)
        selector = jax.vmap(slot_selector)(matched, position)
        row_slots = jax.vmap(dispatch_rows)(token_block, selector)
        cot_slots = jax.vmap(dispatch_rows)(cot_block, selector)
        gate_slots_all = jax.vmap(slot_gates)(weights, selector)
        forward_sum = jnp.zeros((N_MEMBER, EXP_WIN, CAP, D), jnp.float32)
        backward_sum = jnp.zeros((N_MEMBER, EXP_WIN, CAP, D), jnp.float32)
        piece_grads = []
        for expert in range(EXP_WIN):
            row_flat = row_slots[:, expert].reshape(N_MEMBER * CAP, D)
            cot_flat = cot_slots[:, expert].reshape(N_MEMBER * CAP, D)
            gate_flat = gate_slots_all[:, expert].reshape(N_MEMBER * CAP, 1)
            for part_index in range(SPLIT):
                piece_index = expert * SPLIT + part_index
                partial_value, input_part, weight_part = piece_work(row_flat, gate_flat, cot_flat, weights_bf[0, piece_index], weights_bf[1, piece_index], weights_bf[2, piece_index])
                forward_sum = forward_sum.at[:, expert].add(partial_value.astype(jnp.float32).reshape(N_MEMBER, CAP, D))
                backward_sum = backward_sum.at[:, expert].add(input_part.astype(jnp.float32).reshape(N_MEMBER, CAP, D))
                piece_grads.append(weight_part)
        out_block = jax.vmap(collect_rows)(forward_sum, matched, position).astype(jnp.bfloat16)
        grad_block = jax.vmap(collect_rows)(backward_sum, matched, position).astype(jnp.bfloat16)
        grad_sum = grad_sum + jnp.stack(piece_grads, axis=1).astype(jnp.float32)
        return (grad_sum, (out_block, grad_block))
    zero_grads = jnp.zeros((3, PIECES, D, FF_PIECE), jnp.float32)
    gradient, (layer_out, token_grad) = lax.scan(group_step, zero_grads, grouped)
    new_first = beta_one * first_moment + (1.0 - beta_one) * gradient
    new_second = beta_two * second_moment + (1.0 - beta_two) * gradient * gradient
    adam_step = new_first / bias_one / (jnp.sqrt(new_second / bias_two) + adam_eps) + decay_rate * masters
    updated = masters - learn_rate * adam_step
    return (layer_out.reshape(TOKENS, D), token_grad.reshape(TOKENS, D), updated[:2], updated[2], new_first, new_second)
```

```python
import functools

import jax
import jax.numpy as jnp
from jax import lax
from jax.experimental import pallas as pl
from jax.experimental.pallas import tpu as pltpu
from jax.sharding import PartitionSpec as P

MESH = pl.DeviceIdType.MESH
BF = jnp.bfloat16
F32 = jnp.float32
CAP = 80
WIN = 4
TOK = 128
D = 2560
FF = 384
SH = 320
SLOTS = WIN * CAP
ROWS = 16 * CAP
HALF = 2 * CAP

beta_one = 0.9
beta_two = 0.95
learn_rate = 0.0003
decay_rate = 0.1
adam_eps = 1e-08
bias_one = 1.0 - 0.9**10
bias_two = 1.0 - 0.95**10

NN = (((1,), (0,)), ((), ()))
NT = (((1,), (1,)), ((), ()))
TN = (((0,), (0,)), ((), ()))


def dot(a, b, dims):
    return lax.dot_general(a, b, dims, preferred_element_type=F32)


def loop(count, body):
    lax.fori_loop(0, count, lambda i, c: (body(i), c)[1], 0)


def kernel(
    gates,
    tok,
    cot,
    wgu_in,
    wd_in,
    out_ref,
    tgrad_ref,
    ggu_ref,
    gd_ref,
    gates_p,
    tok_p,
    cot_p,
    slots,
    rows,
    cots,
    wgu,
    wd,
    hid,
    dgu,
    pre,
    psend,
    pown,
    precv,
    ret,
    fin_send,
    fin_recv,
    y1gu,
    y1d,
    y2gu,
    y2d,
    xgu,
    xd,
    send_sem,
    recv_sem,
    loc_sem,
    credit,
):
    g = lax.axis_index("group")
    m = lax.axis_index("member")
    xh, y = g // 4, g % 4
    z, xc = m // 4, m % 4
    x, c = xc // 2, xc % 2
    to_core = (g, z * 4 + x * 2 + (1 - c))
    to_x = (g, z * 4 + (1 - x) * 2 + c)

    def at_z(step):
        return (g, ((z + step) % 4) * 4 + xc)

    y_up, y_dn, y_far = (y + 1) % 4, (y + 3) % 4, (y + 2) % 4
    to_yup = (xh * 4 + y_up, m)
    to_ydn = (xh * 4 + y_dn, m)
    to_xh = ((1 - xh) * 4 + y, m)

    used = [0]

    def send(src, dst, target):
        i = used[0]
        used[0] += 1
        copy = pltpu.make_async_remote_copy(
            src_ref=src,
            dst_ref=dst,
            send_sem=send_sem.at[i],
            recv_sem=recv_sem.at[i],
            device_id=target,
            device_id_type=MESH,
        )
        copy.start()
        return copy

    barrier = pltpu.get_barrier_semaphore()
    for other in (to_core, to_x, at_z(1), at_z(2), at_z(3), to_yup, to_ydn, to_xh):
        pl.semaphore_signal(barrier, inc=1, device_id=other, device_id_type=MESH)
    pl.semaphore_wait(barrier, 8)

    def shard(ref, xh_, y_, first=0, count=SH):
        start = pl.multiple_of((xh_ * 4 + y_) * SH + first, 16)
        return ref.at[pl.ds(start, count)]

    def block(ref, dz, dc, dx):
        return ref.at[pl.ds(dz * SLOTS + dc * HALF + dx * CAP, CAP)]

    late = []

    c_gates = send(gates, gates_p, to_x)
    c_tok = send(tok, tok_p, to_x)
    late += [c_gates, c_tok]

    own_w = [
        pltpu.make_async_copy(wgu_in, shard(wgu, xh, y), loc_sem.at[0]),
        pltpu.make_async_copy(wd_in, shard(wd, xh, y), loc_sem.at[1]),
    ]
    for copy in own_w:
        copy.start()

    def w_first(src, buf):
        up = send(src, shard(buf, xh, y), to_yup)
        dn = send(src, shard(buf, xh, y), to_ydn)
        far = send(src, shard(buf, xh, y), to_xh)
        late.extend([up, dn, far])
        return up, dn, far

    def w_second(buf, far):
        far.wait_recv()
        part = shard(buf, 1 - xh, y)
        up = send(part, part, to_yup)
        dn = send(part, part, to_ydn)
        late.extend([up, dn])
        return up, dn

    def w_forward(buf, xh_, up, dn):
        up.wait_recv()
        part = shard(buf, xh_, y_dn, 0, SH // 2)
        on_up = send(part, part, to_yup)
        dn.wait_recv()
        part = shard(buf, xh_, y_up, SH // 2, SH // 2)
        on_dn = send(part, part, to_ydn)
        late.extend([on_up, on_dn])
        return on_up, on_dn

    gu0 = w_first(wgu_in, wgu)

    def fill(mat_ref, val_ref, dst, dx, base, gated):
        mat = mat_ref[...]
        if not gated:
            mat = jnp.where(mat > 0, jnp.ones_like(mat), jnp.zeros_like(mat))

        def tile(n):
            cols = pl.ds(pl.multiple_of(n * 512, 512), 512)
            val = dot(mat, val_ref[:, cols], NN).astype(BF)
            dst[pl.ds(dx * CAP, CAP), cols] = val[:CAP]
            slots[pl.ds(base, 3 * CAP), cols] = val[CAP:]

        loop(D // 512, tile)

    def spread(dst, dx, base):
        sent = {}
        for dz in (1, 3, 2):
            src = slots.at[pl.ds(base + (dz - 1) * CAP, CAP)]
            sent[dz] = send(src, block(dst, dz, 0, dx), at_z(4 - dz))
        return sent

    def cross(dst, dz, dx):
        copy = send(block(dst, dz, 0, dx), block(dst, dz, 1, dx), to_core)
        late.append(copy)
        return copy

    fill(gates, tok, rows, 0, 0, False)
    z_tok0 = spread(rows, 0, 0)
    core_tok, core_cot = {}, {}
    core_tok[0, 0] = cross(rows, 0, 0)

    c_gates.wait_recv()
    c_tok.wait_recv()
    fill(gates_p, tok_p, rows, 1, 3 * CAP, False)
    z_tok1 = spread(rows, 1, 3 * CAP)
    core_tok[0, 1] = cross(rows, 0, 1)
    c_cot = send(cot, cot_p, to_x)
    late.append(c_cot)

    gu1 = w_second(wgu, gu0[2])
    gu2 = w_forward(wgu, xh, gu0[0], gu0[1])
    d0 = w_first(wd_in, wd)

    for dz in (1, 3, 2):
        z_tok0[dz].wait_recv()
        core_tok[dz, 0] = cross(rows, dz, 0)
    for dz in (1, 3, 2):
        z_tok0[dz].wait_send()
    fill(gates, cot, cots, 0, 0, True)
    z_cot0 = spread(cots, 0, 0)
    core_cot[0, 0] = cross(cots, 0, 0)

    gu3 = w_forward(wgu, 1 - xh, gu1[0], gu1[1])
    d1 = w_second(wd, d0[2])
    d2 = w_forward(wd, xh, d0[0], d0[1])

    for dz in (1, 3, 2):
        z_tok1[dz].wait_recv()
        core_tok[dz, 1] = cross(rows, dz, 1)
    for dz in (1, 3, 2):
        z_tok1[dz].wait_send()
    c_cot.wait_recv()
    fill(gates_p, cot_p, cots, 1, 3 * CAP, True)
    z_cot1 = spread(cots, 1, 3 * CAP)
    core_cot[0, 1] = cross(cots, 0, 1)
    d3 = w_forward(wd, 1 - xh, d1[0], d1[1])

    for copy in gu2 + gu3:
        copy.wait_recv()
    for copy in own_w:
        copy.wait()

    def forward_one(dz):
        here = pl.ds(dz * SLOTS, SLOTS)

        def tile(n):
            cols = pl.ds(pl.multiple_of(n * 256, 256), 256)
            pre[:, cols] = dot(rows[here, :], wgu[:, cols], NN)

        loop(3, tile)

        def act(n):
            src = pl.ds(pl.multiple_of(n * 16, 16), 16)
            dst = pl.ds(pl.multiple_of(dz * SLOTS + n * 16, 16), 16)
            gate, up = pre[src, :FF], pre[src, FF:]
            sig = jax.nn.sigmoid(gate)
            active = gate * sig
            hid[dst, :] = (active * up).astype(BF)
            dgu[dst, :FF] = (up * (sig * (1.0 + gate * (1.0 - sig)))).astype(BF)
            dgu[dst, FF:] = active.astype(BF)

        loop(SLOTS // 16, act)

    def core_wait(table, dz):
        table[dz, 0].wait_recv()
        table[dz, 1].wait_recv()

    for dz in (0, 1, 3, 2):
        core_wait(core_tok, dz)
        forward_one(dz)
        if dz == 1:
            for step in (1, 3, 2):
                z_cot0[step].wait_recv()
                core_cot[step, 0] = cross(cots, step, 0)

    for copy in d2 + d3:
        copy.wait_recv()

    def product(left, right, dz, arr):
        here = pl.ds(dz * SLOTS, SLOTS)

        def tile(n):
            cols = pl.ds(pl.multiple_of(n * 256, 256), 256)
            val = dot(left[here, :], right[cols, :], NT).astype(BF)
            pown[pl.ds((arr * 4 + dz) * HALF, HALF), cols] = val[:HALF]
            psend[pl.ds(dz * HALF, HALF), cols] = val[HALF:]

        loop(D // 256, tile)

    def hand_over(dz):
        part = pl.ds(dz * HALF, HALF)
        return send(psend.at[part], precv.at[part], to_core)

    def add_up(dz, arr, copy):
        copy.wait_recv()

        def tile(n):
            k = pl.multiple_of(n * 16, 16)
            a = pown[pl.ds((arr * 4 + dz) * HALF + k, 16), :].astype(F32)
            b = precv[pl.ds(dz * HALF + k, 16), :].astype(F32)
            pown[pl.ds((arr * 4 + dz) * HALF + k, 16), :] = (a + b).astype(BF)

        loop(HALF // 16, tile)

    def give_back(dz, arr):
        got = []
        for dx in (0, 1):
            src = pown.at[pl.ds((arr * 4 + dz) * HALF + dx * CAP, CAP)]
            dst = ret.at[pl.ds((arr * 2 + dx) * SLOTS + dz * CAP, CAP)]
            if dz == 0:
                copy = pltpu.make_async_copy(src, dst, loc_sem.at[2 + arr * 2 + dx])
                copy.start()
            else:
                copy = send(src, dst, at_z(dz))
                late.append(copy)
            got.append(copy)
        return got

    order = (1, 3, 2, 0)
    hand = {}
    back = {}
    for dz in order:
        product(hid, wd, dz, 0)
        hand[dz] = hand_over(dz)
    for dz in order:
        add_up(dz, 0, hand[dz])
        pl.semaphore_signal(credit.at[dz], inc=1, device_id=to_core, device_id_type=MESH)
        back[0, dz] = give_back(dz, 0)

    for dz in (1, 3, 2):
        z_cot1[dz].wait_recv()
        core_cot[dz, 1] = cross(cots, dz, 1)

    def backward_one(dz):
        here = pl.ds(dz * SLOTS, SLOTS)
        pre[:, :FF] = dot(cots[here, :], wd[...], NN)

        def act(n):
            src = pl.ds(pl.multiple_of(n * 16, 16), 16)
            dst = pl.ds(pl.multiple_of(dz * SLOTS + n * 16, 16), 16)
            dh = pre[src, :FF]
            dgu[dst, :FF] = (dgu[dst, :FF].astype(F32) * dh).astype(BF)
            dgu[dst, FF:] = (dgu[dst, FF:].astype(F32) * dh).astype(BF)

        loop(SLOTS // 16, act)

    hand_b = {}
    for dz in order:
        core_wait(core_cot, dz)
        backward_one(dz)
        hand[dz].wait_send()
        pl.semaphore_wait(credit.at[dz], 1)
        product(dgu, wgu, dz, 1)
        hand_b[dz] = hand_over(dz)
    for dz in order:
        add_up(dz, 1, hand_b[dz])
        back[1, dz] = give_back(dz, 1)

    for copy in late:
        copy.wait_send()
    done = len(late)

    def weight_grad(xh_, pair):
        cols = pl.ds(pl.multiple_of((xh_ * 2 + pair) * 2 * SH, 128), 2 * SH)
        where = pl.ds(pl.multiple_of((xh_ * 2 + pair) * 2 * SH, 128), 2 * SH)
        wgu[where, :] = dot(rows[:, cols], dgu[...], TN).astype(BF)
        wd[where, :] = dot(cots[:, cols], hid[...], TN).astype(BF)

    near = y // 2
    loop(2, lambda i: weight_grad(i, 1 - near))
    first = []
    for xh_ in (0, 1):
        for buf, land in ((wgu, y1gu), (wd, y1d)):
            part = shard(buf, xh_, y_far, 0, SH // 2)
            up = send(part, land.at[xh_], to_yup)
            part = shard(buf, xh_, y_far, SH // 2, SH // 2)
            dn = send(part, land.at[2 + xh_], to_ydn)
            late += [up, dn]
            first.append((xh_, buf, land, up, dn))
    loop(2, lambda i: weight_grad(i, near))

    def add_into(buf, start, land, k):
        def tile(n):
            r = pl.multiple_of(n * 16, 16)
            at = pl.ds(pl.multiple_of(start + r, 16), 16)
            a = buf[at, :].astype(F32) + land[k, pl.ds(r, 16), :].astype(F32)
            buf[at, :] = a.astype(BF)

        loop(SH // 2 // 16, tile)

    second = []
    for xh_, buf, land, up, dn in first:
        land2 = y2gu if buf is wgu else y2d
        up.wait_recv()
        add_into(buf, (xh_ * 4 + y_up) * SH, land, xh_)
        on_up = send(shard(buf, xh_, y_up), land2.at[xh_], to_yup)
        dn.wait_recv()
        add_into(buf, (xh_ * 4 + y_dn) * SH + SH // 2, land, 2 + xh_)
        on_dn = send(shard(buf, xh_, y_dn), land2.at[2 + xh_], to_ydn)
        late += [on_up, on_dn]
        second += [on_up, on_dn]

    def combine(arr):
        for copy in back[arr, 0]:
            copy.wait()
        for dz in (1, 3, 2):
            for copy in back[arr, dz]:
                copy.wait_recv()

        def pick(mat):
            if arr == 1:
                mat = jnp.where(mat > 0, jnp.ones_like(mat), jnp.zeros_like(mat))
            return mat

        mat_p = pick(gates_p[...])

        def tile(n):
            cols = pl.ds(pl.multiple_of(n * 512, 512), 512)
            part = ret[pl.ds((arr * 2 + 1) * SLOTS, SLOTS), cols]
            fin_send[arr, :, cols] = dot(mat_p, part, TN).astype(BF)

        loop(D // 512, tile)
        copy = send(fin_send.at[arr], fin_recv.at[arr], to_x)
        late.append(copy)
        return copy, pick(gates[...])

    def finish(arr, copy, mat, dst):
        copy.wait_recv()

        def tile(n):
            cols = pl.ds(pl.multiple_of(n * 512, 512), 512)
            part = ret[pl.ds(arr * 2 * SLOTS, SLOTS), cols]
            total = dot(mat, part, TN) + fin_recv[arr, :, cols].astype(F32)
            dst[:, cols] = total.astype(BF)

        loop(D // 512, tile)

    comb0 = combine(0)

    for copy in second:
        copy.wait_recv()

    def owner_sum(xh_, buf, land):
        start = (xh_ * 4 + y) * SH

        def value(r):
            at = pl.ds(pl.multiple_of(start + r, 16), 16)
            here = pl.ds(r, 16)
            total = buf[at, :].astype(F32) + land[xh_, here, :].astype(F32)
            return total + land[2 + xh_, here, :].astype(F32)

        return start, value

    last = []
    for buf, land, out, recv in ((wgu, y2gu, ggu_ref, xgu), (wd, y2d, gd_ref, xd)):
        start, value = owner_sum(1 - xh, buf, land)

        def tile(n, buf=buf, start=start, value=value):
            r = pl.multiple_of(n * 16, 16)
            buf[pl.ds(pl.multiple_of(start + r, 16), 16), :] = value(r).astype(BF)

        loop(SH // 16, tile)
        copy = send(shard(buf, 1 - xh, y), recv, to_xh)
        late.append(copy)
        last.append(copy)
    finish(0, *comb0, out_ref)
    comb1 = combine(1)
    for copy, (buf, land, out, recv) in zip(
        last, ((wgu, y2gu, ggu_ref, xgu), (wd, y2d, gd_ref, xd))
    ):
        copy.wait_recv()
        start, value = owner_sum(xh, buf, land)

        def tile(n, out=out, value=value, recv=recv):
            r = pl.multiple_of(n * 16, 16)
            out[pl.ds(r, 16), :] = value(r) + recv[pl.ds(r, 16), :].astype(F32)

        loop(SH // 16, tile)
    finish(1, *comb1, tgrad_ref)

    for copy in late[done:]:
        copy.wait_send()
    for copies in (z_cot0, z_cot1):
        for copy in copies.values():
            copy.wait_send()
    for dz in order:
        hand_b[dz].wait_send()
    assert used[0] <= N_COPY, used[0]


N_COPY = 128


def exchange(gates, tok, cot, wgu, wd):
    vmem = pl.BlockSpec(memory_space=pltpu.VMEM)
    shapes = [
        jax.ShapeDtypeStruct((TOK, D), BF),
        jax.ShapeDtypeStruct((TOK, D), BF),
        jax.ShapeDtypeStruct((SH, 2 * FF), F32),
        jax.ShapeDtypeStruct((SH, FF), F32),
    ]
    scratch = [
        pltpu.VMEM((SLOTS, TOK), BF),
        pltpu.VMEM((TOK, D), BF),
        pltpu.VMEM((TOK, D), BF),
        pltpu.VMEM((6 * CAP, D), BF),
        pltpu.VMEM((ROWS, D), BF),
        pltpu.VMEM((ROWS, D), BF),
        pltpu.VMEM((D, 2 * FF), BF),
        pltpu.VMEM((D, FF), BF),
        pltpu.VMEM((ROWS, FF), BF),
        pltpu.VMEM((ROWS, 2 * FF), BF),
        pltpu.VMEM((SLOTS, 2 * FF), F32),
        pltpu.VMEM((4 * HALF, D), BF),
        pltpu.VMEM((8 * HALF, D), BF),
        pltpu.VMEM((4 * HALF, D), BF),
        pltpu.VMEM((4 * SLOTS, D), BF),
        pltpu.VMEM((2, TOK, D), BF),
        pltpu.VMEM((2, TOK, D), BF),
        pltpu.VMEM((4, SH // 2, 2 * FF), BF),
        pltpu.VMEM((4, SH // 2, FF), BF),
        pltpu.VMEM((4, SH, 2 * FF), BF),
        pltpu.VMEM((4, SH, FF), BF),
        pltpu.VMEM((SH, 2 * FF), BF),
        pltpu.VMEM((SH, FF), BF),
        pltpu.SemaphoreType.DMA((N_COPY,)),
        pltpu.SemaphoreType.DMA((N_COPY,)),
        pltpu.SemaphoreType.DMA((6,)),
        pltpu.SemaphoreType.REGULAR((4,)),
    ]
    return pl.pallas_call(
        kernel,
        out_shape=shapes,
        in_specs=[vmem] * 5,
        out_specs=[vmem] * 4,
        scratch_shapes=scratch,
        compiler_params=pltpu.CompilerParams(
            collective_id=0, has_side_effects=True, vmem_limit_bytes=65 * 2**20 - 2**20
        ),
        cost_estimate=pl.CostEstimate(
            flops=18 * ROWS * D * FF, bytes_accessed=2**22, transcendentals=ROWS * FF
        ),
        name="experts",
    )(gates, tok, cot, wgu, wd)


def slot_gates(route_ids, route_gates):
    z = lax.axis_index("member") // 4
    experts = (z - jnp.arange(WIN, dtype=jnp.int32)) % WIN
    hit = route_ids[:, :, None] == experts[None, None, :]
    matched = jnp.any(hit, axis=1)
    weight = jnp.sum(jnp.where(hit, route_gates[:, :, None].astype(F32), 0.0), axis=1)
    position = jnp.cumsum(matched.astype(jnp.int32), axis=0) - 1
    slot = jnp.arange(CAP, dtype=jnp.int32)
    chosen = matched.T[:, None, :] & (position.T[:, None, :] == slot[None, :, None])
    return jnp.where(chosen, weight.T[:, None, :], 0.0).astype(BF).reshape(SLOTS, TOK)


def per_device(
    tokens, route_ids, route_gates, out_grad, proj_in, proj_out, first_moment, second_moment
):
    gates = slot_gates(route_ids, route_gates)
    wgu = jnp.concatenate([proj_in[0, 0], proj_in[1, 0]], axis=1).astype(BF)
    wd = proj_out[0].astype(BF)
    layer_out, token_grad, ggu, gd = exchange(gates, tokens, out_grad, wgu, wd)
    gradient = jnp.stack([ggu[:, :FF], ggu[:, FF:], gd])[:, None]
    masters = jnp.concatenate([proj_in, proj_out[None]], axis=0)
    new_first = beta_one * first_moment + (1.0 - beta_one) * gradient
    new_second = beta_two * second_moment + (1.0 - beta_two) * gradient * gradient
    adam_step = (
        new_first / bias_one / (jnp.sqrt(new_second / bias_two) + adam_eps) + decay_rate * masters
    )
    updated = masters - learn_rate * adam_step
    return (layer_out, token_grad, updated[:2], updated[2], new_first, new_second)


def solution(mesh):
    rows = P(("group", "member"), None)
    return jax.shard_map(
        per_device,
        mesh=mesh,
        in_specs=(
            rows,
            rows,
            rows,
            rows,
            P(None, "member", "group", None),
            P("member", "group", None),
            P(None, "member", "group", None),
            P(None, "member", "group", None),
        ),
        out_specs=(
            rows,
            rows,
            P(None, "member", "group", None),
            P("member", "group", None),
            P(None, "member", "group", None),
            P(None, "member", "group", None),
        ),
        check_vma=False,
    )
```

```python
import functools

import jax
import jax.numpy as jnp
from jax import lax
from jax.experimental import pallas as pl
from jax.experimental.pallas import tpu as pltpu
from jax.sharding import PartitionSpec as P

MESH = pl.DeviceIdType.MESH
BF = jnp.bfloat16
F32 = jnp.float32
CAP = 80
WIN = 4
TOK = 128
D = 2560
FF = 384
SH = 320
SLOTS = WIN * CAP
ROWS = 16 * CAP
HALF = 2 * CAP
CA = 1792
CB = D - CA
A, B = pl.ds(0, CA), pl.ds(CA, CB)

beta_one = 0.9
beta_two = 0.95
learn_rate = 0.0003
decay_rate = 0.1
adam_eps = 1e-08
bias_one = 1.0 - 0.9**10
bias_two = 1.0 - 0.95**10

NN = (((1,), (0,)), ((), ()))
NT = (((1,), (1,)), ((), ()))
TN = (((0,), (0,)), ((), ()))


def dot(a, b, dims):
    return lax.dot_general(a, b, dims, preferred_element_type=F32)


def loop(count, body):
    lax.fori_loop(0, count, lambda i, c: (body(i), c)[1], 0)


def kernel(
    gates,
    tok,
    cot,
    wgu_in,
    wd_in,
    out_ref,
    tgrad_ref,
    ggu_ref,
    gd_ref,
    gates_p,
    tok_p,
    cot_p,
    slots,
    rows,
    cots,
    wgu,
    wd,
    hid,
    dgu,
    pre,
    psend,
    pown,
    precv,
    ret,
    fin_send,
    fin_recv,
    xret,
    y1gu,
    y1d,
    y2gu,
    y2d,
    xgu,
    xd,
    send_sem,
    recv_sem,
    loc_sem,
    credit,
):
    g = lax.axis_index("group")
    m = lax.axis_index("member")
    xh, y = g // 4, g % 4
    z, xc = m // 4, m % 4
    x, c = xc // 2, xc % 2
    to_core = (g, z * 4 + x * 2 + (1 - c))
    to_x = (g, z * 4 + (1 - x) * 2 + c)

    def at_z(step):
        return (g, ((z + step) % 4) * 4 + xc)

    y_up, y_dn, y_far = (y + 1) % 4, (y + 3) % 4, (y + 2) % 4
    to_yup = (xh * 4 + y_up, m)
    to_ydn = (xh * 4 + y_dn, m)
    to_xh = ((1 - xh) * 4 + y, m)

    used = [0]

    def send(src, dst, target):
        i = used[0]
        used[0] += 1
        copy = pltpu.make_async_remote_copy(
            src_ref=src,
            dst_ref=dst,
            send_sem=send_sem.at[i],
            recv_sem=recv_sem.at[i],
            device_id=target,
            device_id_type=MESH,
        )
        copy.start()
        return copy

    barrier = pltpu.get_barrier_semaphore()
    for other in (to_core, to_x, at_z(1), at_z(2), at_z(3), to_yup, to_ydn, to_xh):
        pl.semaphore_signal(barrier, inc=1, device_id=other, device_id_type=MESH)
    pl.semaphore_wait(barrier, 8)

    def shard(ref, xh_, y_, first=0, count=SH):
        start = pl.multiple_of((xh_ * 4 + y_) * SH + first, 16)
        return ref.at[pl.ds(start, count)]

    def block(ref, dz, dc, dx):
        return ref.at[pl.ds(dz * SLOTS + dc * HALF + dx * CAP, CAP)]

    late = []

    c_gates = send(gates, gates_p, to_x)
    c_tok = send(tok.at[:, A], tok_p, to_x)
    late += [c_gates, c_tok]

    own_w = [
        pltpu.make_async_copy(wgu_in, shard(wgu, xh, y), loc_sem.at[0]),
        pltpu.make_async_copy(wd_in, shard(wd, xh, y), loc_sem.at[1]),
    ]
    for copy in own_w:
        copy.start()

    w_sent = []

    def w_first(src, buf):
        up = send(src, shard(buf, xh, y), to_yup)
        dn = send(src, shard(buf, xh, y), to_ydn)
        late.extend([up, dn])
        return up, dn

    def w_far(src, buf):
        far = send(src, shard(buf, xh, y), to_xh)
        late.append(far)
        return far

    def w_second(buf, far):
        far.wait_recv()
        part = shard(buf, 1 - xh, y)
        up = send(part, part, to_yup)
        dn = send(part, part, to_ydn)
        w_sent.extend([up, dn])
        return up, dn

    def w_forward(buf, xh_, pair):
        up, dn = pair
        up.wait_recv()
        part = shard(buf, xh_, y_dn, 0, SH // 2)
        on_up = send(part, part, to_yup)
        dn.wait_recv()
        part = shard(buf, xh_, y_up, SH // 2, SH // 2)
        on_dn = send(part, part, to_ydn)
        w_sent.extend([on_up, on_dn])
        return on_up, on_dn

    gu0 = w_first(wgu_in, wgu)
    gu_far = w_far(wgu_in, wgu)
    d0 = w_first(wd_in, wd)

    def fill(mat_ref, val_ref, dst, dx, base, gated, width, step):
        mat = mat_ref[...]
        if not gated:
            mat = jnp.where(mat > 0, jnp.ones_like(mat), jnp.zeros_like(mat))

        def tile(n):
            cols = pl.ds(pl.multiple_of(n * step, 128), step)
            val = dot(mat, val_ref[:, cols], NN).astype(BF)
            dst[pl.ds(dx * CAP, CAP), cols] = val[:CAP]
            slots[pl.ds(base * 3 * CAP, 3 * CAP), cols] = val[CAP:]

        loop(width // step, tile)

    def spread(dst, dx, base, dz):
        src = slots.at[pl.ds((base * 3 + dz - 1) * CAP, CAP)]
        land = block(dst, dz, 0, dx)
        if dx == 1:
            src, land = src.at[:, A], land.at[:, A]
        copy = send(src, land, at_z(4 - dz))
        late.append(copy)
        return copy

    def cross(dst, dz, dx, cols):
        copy = send(
            block(dst, dz, 0, dx).at[:, cols], block(dst, dz, 1, dx).at[:, cols], to_core
        )
        late.append(copy)
        return copy

    def own_in(dst, table, dz):
        table[dz, 0] = cross(dst, dz, 0, pl.ds(0, D))
        copy = send(block(dst, dz, 0, 0).at[:, B], block(dst, dz, 0, 1).at[:, B], to_x)
        late.append(copy)
        table[dz, "x"] = copy

    def last_in(dst, table, dz):
        table[dz, "x"].wait_recv()
        table[dz, 2] = cross(dst, dz, 1, B)

    core_tok, core_cot = {}, {}
    fill(gates, tok, rows, 0, 0, False, D, 512)
    z_tok0 = {dz: spread(rows, 0, 0, dz) for dz in (1, 3, 2)}
    own_in(rows, core_tok, 0)
    fill(gates, cot, cots, 0, 2, True, D, 512)
    gu2 = w_forward(wgu, xh, gu0)
    d2 = w_forward(wd, xh, d0)

    c_gates.wait_recv()
    c_tok.wait_recv()
    fill(gates_p, tok_p, rows, 1, 1, False, CA, 896)
    z_tok1 = {dz: spread(rows, 1, 1, dz) for dz in (1, 3, 2)}
    core_tok[0, 1] = cross(rows, 0, 1, A)
    for dz in (1, 3, 2):
        z_tok0[dz].wait_recv()
        own_in(rows, core_tok, dz)
    c_cot = send(cot.at[:, A], cot_p, to_x)
    late.append(c_cot)
    d_far = w_far(wd_in, wd)
    z_cot0 = {dz: spread(cots, 0, 2, dz) for dz in (1, 3)}
    gu1 = w_second(wgu, gu_far)
    z_cot0[2] = spread(cots, 0, 2, 2)
    last_in(rows, core_tok, 0)
    own_in(cots, core_cot, 0)
    for dz in (1, 3, 2):
        z_tok1[dz].wait_recv()
        core_tok[dz, 1] = cross(rows, dz, 1, A)
        last_in(rows, core_tok, dz)
    c_cot.wait_recv()
    fill(gates_p, cot_p, cots, 1, 3, True, CA, 896)
    z_cot1 = {dz: spread(cots, 1, 3, dz) for dz in (1, 3)}
    core_cot[0, 1] = cross(cots, 0, 1, A)
    gu3 = w_forward(wgu, 1 - xh, gu1)
    d1 = w_second(wd, d_far)
    z_cot1[2] = spread(cots, 1, 3, 2)
    last_in(cots, core_cot, 0)

    for copy in gu2 + gu3:
        copy.wait_recv()
    for copy in own_w:
        copy.wait()

    def forward_one(dz):
        here = pl.ds(dz * SLOTS, SLOTS)

        def tile(n):
            cols = pl.ds(pl.multiple_of(n * 256, 256), 256)
            pre[:, cols] = dot(rows[here, :], wgu[:, cols], NN)

        loop(3, tile)

        def act(n):
            src = pl.ds(pl.multiple_of(n * 16, 16), 16)
            dst = pl.ds(pl.multiple_of(dz * SLOTS + n * 16, 16), 16)
            gate, up = pre[src, :FF], pre[src, FF:]
            sig = jax.nn.sigmoid(gate)
            active = gate * sig
            hid[dst, :] = (active * up).astype(BF)
            dgu[dst, :FF] = (up * (sig * (1.0 + gate * (1.0 - sig)))).astype(BF)
            dgu[dst, FF:] = active.astype(BF)

        loop(SLOTS // 16, act)

    def core_wait(table, dz):
        for part in range(3):
            table[dz, part].wait_recv()

    def cot_one(dz):
        z_cot0[dz].wait_recv()
        own_in(cots, core_cot, dz)

    def cot_two(dz):
        z_cot1[dz].wait_recv()
        core_cot[dz, 1] = cross(cots, dz, 1, A)
        last_in(cots, core_cot, dz)

    core_wait(core_tok, 0)
    forward_one(0)
    d3 = w_forward(wd, 1 - xh, d1)
    core_wait(core_tok, 1)
    forward_one(1)
    cot_one(1)
    cot_one(3)
    core_wait(core_tok, 3)
    forward_one(3)
    cot_one(2)
    core_wait(core_tok, 2)
    forward_one(2)

    for copy in d2 + d3:
        copy.wait_recv()

    def product(left, right, dz, arr):
        here = pl.ds(dz * SLOTS, SLOTS)

        def tile(n):
            cols = pl.ds(pl.multiple_of(n * 512, 512), 512)
            val = dot(left[here, :], right[cols, :], NT).astype(BF)
            pown[pl.ds((arr * 4 + dz) * HALF, HALF), cols] = val[:HALF]
            psend[pl.ds(dz * HALF, HALF), cols] = val[HALF:]

        loop(D // 512, tile)

    def hand_over(dz):
        part = pl.ds(dz * HALF, HALF)
        return send(psend.at[part], precv.at[part], to_core)

    def add_up(dz, arr, copy):
        copy.wait_recv()

        def tile(n):
            k = pl.multiple_of(n * 16, 16)
            a = pown[pl.ds((arr * 4 + dz) * HALF + k, 16), :].astype(F32)
            b = precv[pl.ds(dz * HALF + k, 16), :].astype(F32)
            pown[pl.ds((arr * 4 + dz) * HALF + k, 16), :] = (a + b).astype(BF)

        loop(HALF // 16, tile)

    def swap(dz, arr):
        src = pown.at[pl.ds((arr * 4 + dz) * HALF + CAP, CAP), B]
        copy = send(src, xret.at[pl.ds((arr * 4 + dz) * CAP, CAP)], to_x)
        late.append(copy)
        swapped[arr, dz] = copy

    def add_swapped(dz, arr):
        swapped[arr, dz].wait_recv()
        a = pown[pl.ds((arr * 4 + dz) * HALF, CAP), CA:].astype(F32)
        b = xret[pl.ds((arr * 4 + dz) * CAP, CAP), :].astype(F32)
        pown[pl.ds((arr * 4 + dz) * HALF, CAP), CA:] = (a + b).astype(BF)

    def give_part(dz, arr, dx, cols, sem):
        src = pown.at[pl.ds((arr * 4 + dz) * HALF + dx * CAP, CAP), cols]
        dst = ret.at[pl.ds((arr * 2 + dx) * SLOTS + dz * CAP, CAP), cols]
        if dz == 0:
            copy = pltpu.make_async_copy(src, dst, loc_sem.at[2 + arr * 3 + sem])
            copy.start()
        else:
            copy = send(src, dst, at_z(dz))
            late.append(copy)
        return copy

    def give_back(dz, arr):
        back[arr, dz] = [give_part(dz, arr, dx, A, dx) for dx in (0, 1)]

    def give_last(dz, arr):
        add_swapped(dz, arr)
        back[arr, dz].append(give_part(dz, arr, 0, B, 2))

    order = (0, 1, 3, 2)
    hand, hand_b = {}, {}
    back, swapped = {}, {}
    for dz in order:
        product(hid, wd, dz, 0)
        hand[dz] = hand_over(dz)
    cot_two(1)
    cot_two(3)
    for dz in order:
        add_up(dz, 0, hand[dz])
        swap(dz, 0)
        pl.semaphore_signal(credit.at[dz], inc=1, device_id=to_core, device_id_type=MESH)

    def backward_one(dz):
        core_wait(core_cot, dz)
        here = pl.ds(dz * SLOTS, SLOTS)
        pre[:, :FF] = dot(cots[here, :], wd[...], NN)

        def act(n):
            src = pl.ds(pl.multiple_of(n * 16, 16), 16)
            dst = pl.ds(pl.multiple_of(dz * SLOTS + n * 16, 16), 16)
            dh = pre[src, :FF]
            dgu[dst, :FF] = (dgu[dst, :FF].astype(F32) * dh).astype(BF)
            dgu[dst, FF:] = (dgu[dst, FF:].astype(F32) * dh).astype(BF)

        loop(SLOTS // 16, act)

    def backward_two(dz):
        hand[dz].wait_send()
        pl.semaphore_wait(credit.at[dz], 1)
        product(dgu, wgu, dz, 1)
        hand_b[dz] = hand_over(dz)

    for dz in (0, 1, 3):
        backward_one(dz)
        backward_two(dz)
    cot_two(2)
    for dz in (1, 3, 2, 0):
        give_back(dz, 0)
    backward_one(2)

    for copy in w_sent:
        copy.wait_send()

    near = y // 2
    other = 1 - xh

    def weight_grad(left, right, buf, xh_, pair):
        at = pl.ds(pl.multiple_of((xh_ * 2 + pair) * 2 * SH, 128), 2 * SH)
        buf[at, :] = dot(left[:, at], right[...], TN).astype(BF)

    def add_into(buf, start, land, k):
        def tile(n):
            r = pl.multiple_of(n * 16, 16)
            at = pl.ds(pl.multiple_of(start + r, 16), 16)
            a = buf[at, :].astype(F32) + land[k, pl.ds(r, 16), :].astype(F32)
            buf[at, :] = a.astype(BF)

        loop(SH // 2 // 16, tile)

    def ring_first(buf, land, k, xh_):
        up = send(shard(buf, xh_, y_far, 0, SH // 2), land.at[k], to_yup)
        dn = send(shard(buf, xh_, y_far, SH // 2, SH // 2), land.at[2 + k], to_ydn)
        late.extend([up, dn])
        return up, dn

    def ring_second(buf, land, land2, k, xh_, pair):
        up, dn = pair
        up.wait_recv()
        add_into(buf, (xh_ * 4 + y_up) * SH, land, k)
        on_up = send(shard(buf, xh_, y_up), land2.at[k], to_yup)
        dn.wait_recv()
        add_into(buf, (xh_ * 4 + y_dn) * SH + SH // 2, land, 2 + k)
        on_dn = send(shard(buf, xh_, y_dn), land2.at[2 + k], to_ydn)
        late.extend([on_up, on_dn])
        return on_up, on_dn

    def owner_value(buf, land, k, xh_):
        start = (xh_ * 4 + y) * SH

        def value(r):
            at = pl.ds(pl.multiple_of(start + r, 16), 16)
            here = pl.ds(r, 16)
            total = buf[at, :].astype(F32) + land[k, here, :].astype(F32)
            return total + land[2 + k, here, :].astype(F32)

        return start, value

    def ring_third(buf, land, recv, pair):
        for copy in pair:
            copy.wait_recv()
        start, value = owner_value(buf, land, 0, other)

        def tile(n):
            r = pl.multiple_of(n * 16, 16)
            buf[pl.ds(pl.multiple_of(start + r, 16), 16), :] = value(r).astype(BF)

        loop(SH // 16, tile)
        copy = send(shard(buf, other, y), recv, to_xh)
        late.append(copy)
        return copy

    def ring_last(buf, land, recv, out, pair, copy):
        for c_ in pair:
            c_.wait_recv()
        copy.wait_recv()
        _, value = owner_value(buf, land, 1, xh)

        def tile(n):
            r = pl.multiple_of(n * 16, 16)
            out[pl.ds(r, 16), :] = value(r) + recv[pl.ds(r, 16), :].astype(F32)

        loop(SH // 16, tile)

    weight_grad(cots, hid, wd, other, 1 - near)
    d_a = ring_first(wd, y1d, 0, other)
    weight_grad(cots, hid, wd, xh, 1 - near)
    d_b = ring_first(wd, y1d, 1, xh)
    weight_grad(cots, hid, wd, other, near)
    weight_grad(cots, hid, wd, xh, near)
    backward_two(2)
    for dz in (1, 3, 0):
        add_up(dz, 1, hand_b[dz])
        swap(dz, 1)
    for dz in (1, 3, 2, 0):
        give_last(dz, 0)
    weight_grad(rows, dgu, wgu, other, 1 - near)
    gu_a = ring_first(wgu, y1gu, 0, other)
    d_a = ring_second(wd, y1d, y2d, 0, other, d_a)
    weight_grad(rows, dgu, wgu, xh, 1 - near)
    gu_b = ring_first(wgu, y1gu, 1, xh)
    d_b = ring_second(wd, y1d, y2d, 1, xh, d_b)
    weight_grad(rows, dgu, wgu, other, near)
    gu_a = ring_second(wgu, y1gu, y2gu, 0, other, gu_a)
    weight_grad(rows, dgu, wgu, xh, near)
    gu_b = ring_second(wgu, y1gu, y2gu, 1, xh, gu_b)
    add_up(2, 1, hand_b[2])
    swap(2, 1)
    for dz in (1, 3, 2, 0):
        give_back(dz, 1)
    d_x = ring_third(wd, y2d, xd, d_a)
    for dz in (1, 3, 2, 0):
        give_last(dz, 1)
    gu_x = ring_third(wgu, y2gu, xgu, gu_a)

    def combine(arr):
        for copy in back[arr, 0]:
            copy.wait()
        for dz in (1, 3, 2):
            for copy in back[arr, dz][:2]:
                copy.wait_recv()

        def pick(mat):
            if arr == 1:
                mat = jnp.where(mat > 0, jnp.ones_like(mat), jnp.zeros_like(mat))
            return mat

        mat_p = pick(gates_p[...])

        def tile(n):
            cols = pl.ds(pl.multiple_of(n * 896, 128), 896)
            part = ret[pl.ds((arr * 2 + 1) * SLOTS, SLOTS), cols]
            fin_send[arr, :, cols] = dot(mat_p, part, TN).astype(BF)

        loop(CA // 896, tile)
        copy = send(fin_send.at[arr], fin_recv.at[arr], to_x)
        late.append(copy)
        return copy, pick(gates[...])

    def finish(arr, copy, mat, dst):
        for dz in (1, 3, 2):
            back[arr, dz][2].wait_recv()
        part = ret[pl.ds(arr * 2 * SLOTS, SLOTS), CA:]
        dst[:, CA:] = dot(mat, part, TN).astype(BF)
        copy.wait_recv()

        def tile(n):
            cols = pl.ds(pl.multiple_of(n * 896, 128), 896)
            part = ret[pl.ds(arr * 2 * SLOTS, SLOTS), cols]
            total = dot(mat, part, TN) + fin_recv[arr, :, cols].astype(F32)
            dst[:, cols] = total.astype(BF)

        loop(CA // 896, tile)

    comb0 = combine(0)
    ring_last(wd, y2d, xd, gd_ref, d_b, d_x)
    finish(0, *comb0, out_ref)
    comb1 = combine(1)
    ring_last(wgu, y2gu, xgu, ggu_ref, gu_b, gu_x)
    finish(1, *comb1, tgrad_ref)

    for copy in late:
        copy.wait_send()
    for dz in order:
        hand_b[dz].wait_send()
    assert used[0] <= N_COPY, used[0]


N_COPY = 160


def exchange(gates, tok, cot, wgu, wd):
    vmem = pl.BlockSpec(memory_space=pltpu.VMEM)
    shapes = [
        jax.ShapeDtypeStruct((TOK, D), BF),
        jax.ShapeDtypeStruct((TOK, D), BF),
        jax.ShapeDtypeStruct((SH, 2 * FF), F32),
        jax.ShapeDtypeStruct((SH, FF), F32),
    ]
    scratch = [
        pltpu.VMEM((SLOTS, TOK), BF),
        pltpu.VMEM((TOK, CA), BF),
        pltpu.VMEM((TOK, CA), BF),
        pltpu.VMEM((12 * CAP, D), BF),
        pltpu.VMEM((ROWS, D), BF),
        pltpu.VMEM((ROWS, D), BF),
        pltpu.VMEM((D, 2 * FF), BF),
        pltpu.VMEM((D, FF), BF),
        pltpu.VMEM((ROWS, FF), BF),
        pltpu.VMEM((ROWS, 2 * FF), BF),
        pltpu.VMEM((SLOTS, 2 * FF), F32),
        pltpu.VMEM((4 * HALF, D), BF),
        pltpu.VMEM((8 * HALF, D), BF),
        pltpu.VMEM((4 * HALF, D), BF),
        pltpu.VMEM((4 * SLOTS, D), BF),
        pltpu.VMEM((2, TOK, CA), BF),
        pltpu.VMEM((2, TOK, CA), BF),
        pltpu.VMEM((2 * SLOTS, CB), BF),
        pltpu.VMEM((4, SH // 2, 2 * FF), BF),
        pltpu.VMEM((4, SH // 2, FF), BF),
        pltpu.VMEM((4, SH, 2 * FF), BF),
        pltpu.VMEM((4, SH, FF), BF),
        pltpu.VMEM((SH, 2 * FF), BF),
        pltpu.VMEM((SH, FF), BF),
        pltpu.SemaphoreType.DMA((N_COPY,)),
        pltpu.SemaphoreType.DMA((N_COPY,)),
        pltpu.SemaphoreType.DMA((8,)),
        pltpu.SemaphoreType.REGULAR((4,)),
    ]
    return pl.pallas_call(
        kernel,
        out_shape=shapes,
        in_specs=[vmem] * 5,
        out_specs=[vmem] * 4,
        scratch_shapes=scratch,
        compiler_params=pltpu.CompilerParams(
            collective_id=0, has_side_effects=True, vmem_limit_bytes=65 * 2**20 - 2**20
        ),
        cost_estimate=pl.CostEstimate(
            flops=18 * ROWS * D * FF, bytes_accessed=2**22, transcendentals=ROWS * FF
        ),
        name="experts",
    )(gates, tok, cot, wgu, wd)


def slot_gates(route_ids, route_gates):
    z = lax.axis_index("member") // 4
    experts = (z - jnp.arange(WIN, dtype=jnp.int32)) % WIN
    hit = route_ids[:, :, None] == experts[None, None, :]
    matched = jnp.any(hit, axis=1)
    weight = jnp.sum(jnp.where(hit, route_gates[:, :, None].astype(F32), 0.0), axis=1)
    position = jnp.cumsum(matched.astype(jnp.int32), axis=0) - 1
    slot = jnp.arange(CAP, dtype=jnp.int32)
    chosen = matched.T[:, None, :] & (position.T[:, None, :] == slot[None, :, None])
    return jnp.where(chosen, weight.T[:, None, :], 0.0).astype(BF).reshape(SLOTS, TOK)


def per_device(
    tokens, route_ids, route_gates, out_grad, proj_in, proj_out, first_moment, second_moment
):
    gates = slot_gates(route_ids, route_gates)
    wgu = jnp.concatenate([proj_in[0, 0], proj_in[1, 0]], axis=1).astype(BF)
    wd = proj_out[0].astype(BF)
    layer_out, token_grad, ggu, gd = exchange(gates, tokens, out_grad, wgu, wd)
    gradient = jnp.stack([ggu[:, :FF], ggu[:, FF:], gd])[:, None]
    masters = jnp.concatenate([proj_in, proj_out[None]], axis=0)
    new_first = beta_one * first_moment + (1.0 - beta_one) * gradient
    new_second = beta_two * second_moment + (1.0 - beta_two) * gradient * gradient
    adam_step = (
        new_first / bias_one / (jnp.sqrt(new_second / bias_two) + adam_eps) + decay_rate * masters
    )
    updated = masters - learn_rate * adam_step
    return (layer_out, token_grad, updated[:2], updated[2], new_first, new_second)


def solution(mesh):
    rows = P(("group", "member"), None)
    return jax.shard_map(
        per_device,
        mesh=mesh,
        in_specs=(
            rows,
            rows,
            rows,
            rows,
            P(None, "member", "group", None),
            P("member", "group", None),
            P(None, "member", "group", None),
            P(None, "member", "group", None),
        ),
        out_specs=(
            rows,
            rows,
            P(None, "member", "group", None),
            P("member", "group", None),
            P(None, "member", "group", None),
            P(None, "member", "group", None),
        ),
        check_vma=False,
    )
```

```python
import functools

import jax
import jax.numpy as jnp
from jax import lax
from jax.experimental import pallas as pl
from jax.experimental.pallas import tpu as pltpu
from jax.sharding import PartitionSpec as P

MESH = pl.DeviceIdType.MESH
BF = jnp.bfloat16
F32 = jnp.float32
CAP = 80
WIN = 4
TOK = 128
D = 2560
FF = 384
SH = 320
SLOTS = WIN * CAP
ROWS = 16 * CAP
HALF = 2 * CAP
CA = 1792
CB = D - CA
A, B = pl.ds(0, CA), pl.ds(CA, CB)

beta_one = 0.9
beta_two = 0.95
learn_rate = 0.0003
decay_rate = 0.1
adam_eps = 1e-08
bias_one = 1.0 - 0.9**10
bias_two = 1.0 - 0.95**10

NN = (((1,), (0,)), ((), ()))
NT = (((1,), (1,)), ((), ()))
TN = (((0,), (0,)), ((), ()))


def dot(a, b, dims):
    return lax.dot_general(a, b, dims, preferred_element_type=F32)


def loop(count, body):
    lax.fori_loop(0, count, lambda i, c: (body(i), c)[1], 0)


def slot_gates(z, ids_ref, gate_ref, gates):
    ids = ids_ref[...]
    value = gate_ref[...].astype(F32)
    down = lax.broadcasted_iota(jnp.int32, (TOK, TOK), 0)
    lane = lax.broadcasted_iota(jnp.int32, (TOK, TOK), 1)
    row = lax.broadcasted_iota(jnp.int32, (8, TOK), 0)
    named = jnp.zeros((8, TOK), F32)
    match, weight = [], []
    for dz in range(WIN):
        hit = ids == (z - dz + WIN) % WIN
        match.append(jnp.sum(jnp.where(hit, 1.0, 0.0), axis=0, keepdims=True))
        weight.append(jnp.sum(jnp.where(hit, value, 0.0), axis=0, keepdims=True))
        named = jnp.where(row == dz, match[dz], named)
    upto = jnp.where(down <= lane, 1.0, 0.0).astype(BF)
    count = dot(named.astype(BF), upto, NN).astype(jnp.int32)
    slot = lax.broadcasted_iota(jnp.int32, (CAP, TOK), 0)
    for dz in range(WIN):
        place = jnp.where(match[dz] > 0, count[dz : dz + 1] - 1, -1)
        gates[pl.ds(dz * CAP, CAP), :] = jnp.where(slot == place, weight[dz], 0.0).astype(BF)


def kernel(
    ids_ref,
    gate_ref,
    tok_hbm,
    cot_hbm,
    proj_in,
    proj_out,
    out_ref,
    tgrad_ref,
    ggu_ref,
    gd_ref,
    gates,
    gates_p,
    tok_p,
    cot_p,
    slots,
    slots_p,
    rows,
    cots,
    wgu,
    wd,
    hid,
    dgu,
    psend,
    pown,
    precv,
    ret,
    fin_recv,
    xret,
    ggu,
    gd,
    y1gu,
    y1d,
    y2gu,
    y2d,
    xgu,
    xd,
    send_sem,
    recv_sem,
    loc_sem,
    credit,
):
    tok, cot, pre = out_ref, tgrad_ref, ggu_ref
    g = lax.axis_index("group")
    m = lax.axis_index("member")
    xh, y = g // 4, g % 4
    z, xc = m // 4, m % 4
    x, c = xc // 2, xc % 2
    to_core = (g, z * 4 + x * 2 + (1 - c))
    to_x = (g, z * 4 + (1 - x) * 2 + c)

    def at_z(step):
        return (g, ((z + step) % 4) * 4 + xc)

    y_up, y_dn, y_far = (y + 1) % 4, (y + 3) % 4, (y + 2) % 4
    to_yup = (xh * 4 + y_up, m)
    to_ydn = (xh * 4 + y_dn, m)
    to_xh = ((1 - xh) * 4 + y, m)

    used = [0]

    def send(src, dst, target):
        i = used[0]
        used[0] += 1
        copy = pltpu.make_async_remote_copy(
            src_ref=src,
            dst_ref=dst,
            send_sem=send_sem.at[i],
            recv_sem=recv_sem.at[i],
            device_id=target,
            device_id_type=MESH,
        )
        copy.start()
        return copy

    loads = [
        pltpu.make_async_copy(tok_hbm, tok, loc_sem.at[8]),
        pltpu.make_async_copy(proj_in.at[0, 0], pre.at[:, pl.ds(0, FF)], loc_sem.at[9]),
        pltpu.make_async_copy(proj_in.at[1, 0], pre.at[:, pl.ds(FF, FF)], loc_sem.at[10]),
        pltpu.make_async_copy(proj_out.at[0], gd_ref, loc_sem.at[11]),
        pltpu.make_async_copy(cot_hbm, cot, loc_sem.at[12]),
    ]
    for copy in loads:
        copy.start()
    barrier = pltpu.get_barrier_semaphore()
    for other in (to_core, to_x, at_z(1), at_z(2), at_z(3), to_yup, to_ydn, to_xh):
        pl.semaphore_signal(barrier, inc=1, device_id=other, device_id_type=MESH)
    slot_gates(z, ids_ref, gate_ref, gates)
    for copy in loads[:4]:
        copy.wait()
    own = pl.ds(pl.multiple_of((xh * 4 + y) * SH, SH), SH)
    wgu[own, :] = pre[...].astype(BF)
    wd[own, :] = gd_ref[...].astype(BF)
    pl.semaphore_wait(barrier, 8)

    def shard(ref, xh_, y_, first=0, count=SH):
        start = pl.multiple_of((xh_ * 4 + y_) * SH + first, 16)
        return ref.at[pl.ds(start, count)]

    def block(ref, dz, dc, dx):
        return ref.at[pl.ds(dz * SLOTS + dc * HALF + dx * CAP, CAP)]

    late = []

    c_gates = send(gates, gates_p, to_x)
    late.append(c_gates)

    def w_first(buf):
        part = shard(buf, xh, y)
        up = send(part, part, to_yup)
        dn = send(part, part, to_ydn)
        late.extend([up, dn])
        return up, dn

    def w_far(buf):
        far = send(shard(buf, xh, y), shard(buf, xh, y), to_xh)
        late.append(far)
        return far

    def w_second(buf, far):
        far.wait_recv()
        part = shard(buf, 1 - xh, y)
        up = send(part, part, to_yup)
        dn = send(part, part, to_ydn)
        late.extend([up, dn])
        return up, dn

    def w_forward(buf, xh_, pair):
        up, dn = pair
        up.wait_recv()
        part = shard(buf, xh_, y_dn, 0, SH // 2)
        on_up = send(part, part, to_yup)
        dn.wait_recv()
        part = shard(buf, xh_, y_up, SH // 2, SH // 2)
        on_dn = send(part, part, to_ydn)
        late.extend([on_up, on_dn])
        return on_up, on_dn

    gu0 = w_first(wgu)
    gu_far = w_far(wgu)

    def fill(mat_ref, val_ref, dst, dx, base, gated, width, step):
        held = (slots, slots_p)[dx]
        mat = mat_ref[...]
        if not gated:
            mat = jnp.where(mat > 0, jnp.ones_like(mat), jnp.zeros_like(mat))

        def tile(n):
            cols = pl.ds(pl.multiple_of(n * step, 128), step)
            val = dot(mat, val_ref[:, cols], NN).astype(BF)
            dst[pl.ds(dx * CAP, CAP), cols] = val[:CAP]
            held[pl.ds(base * 3 * CAP, 3 * CAP), cols] = val[CAP:]

        loop(width // step, tile)

    def spread(dst, dx, base, dz):
        src = (slots, slots_p)[dx].at[pl.ds((base * 3 + dz - 1) * CAP, CAP)]
        land = block(dst, dz, 0, dx)
        if dx == 1:
            land = land.at[:, A]
        copy = send(src, land, at_z(4 - dz))
        late.append(copy)
        return copy

    def cross(dst, dz, dx, cols):
        copy = send(
            block(dst, dz, 0, dx).at[:, cols], block(dst, dz, 1, dx).at[:, cols], to_core
        )
        late.append(copy)
        return copy

    def own_in(dst, table, dz):
        table[dz, 0] = cross(dst, dz, 0, pl.ds(0, D))

    def own_on(dst, table, dz):
        copy = send(block(dst, dz, 0, 0).at[:, B], block(dst, dz, 0, 1).at[:, B], to_x)
        late.append(copy)
        table[dz, "x"] = copy

    def last_in(dst, table, dz):
        table[dz, "x"].wait_recv()
        table[dz, 2] = cross(dst, dz, 1, B)

    core_tok, core_cot = {}, {}
    fill(gates, tok, rows, 0, 0, False, D, 512)
    z_tok0 = {dz: spread(rows, 0, 0, dz) for dz in (1, 3, 2)}
    own_in(rows, core_tok, 0)
    c_tok = send(tok.at[:, A], tok_p, to_x)
    loads[4].wait()
    fill(gates, cot, cots, 0, 1, True, D, 512)
    gu2 = w_forward(wgu, xh, gu0)
    gu1 = w_second(wgu, gu_far)
    for dz in (1, 3, 2):
        z_tok0[dz].wait_recv()
        own_in(rows, core_tok, dz)
    z_cot0 = {2: spread(cots, 0, 1, 2)}
    c_gates.wait_recv()
    c_tok.wait_recv()
    for dz in (0, 1, 3, 2):
        own_on(rows, core_tok, dz)
    fill(gates_p, tok_p, rows, 1, 0, False, CA, 896)
    z_tok1 = {dz: spread(rows, 1, 0, dz) for dz in (1, 3, 2)}
    core_tok[0, 1] = cross(rows, 0, 1, A)
    d0 = w_first(wd)
    d_far = w_far(wd)
    gu3 = w_forward(wgu, 1 - xh, gu1)
    c_cot = send(cot.at[:, A], cot_p, to_x)
    z_cot0[1] = spread(cots, 0, 1, 1)
    z_cot0[3] = spread(cots, 0, 1, 3)
    d2 = w_forward(wd, xh, d0)
    d1 = w_second(wd, d_far)
    last_in(rows, core_tok, 0)
    own_in(cots, core_cot, 0)
    own_on(cots, core_cot, 0)
    for dz in (1, 3, 2):
        z_tok1[dz].wait_recv()
        core_tok[dz, 1] = cross(rows, dz, 1, A)
    for dz in (1, 3, 2):
        last_in(rows, core_tok, dz)

    for copy in gu2 + gu3:
        copy.wait_recv()

    def forward_one(dz):
        here = pl.ds(dz * SLOTS, SLOTS)

        pre[...] = dot(rows[here, :], wgu[...], NN)

        def act(n):
            src = pl.ds(pl.multiple_of(n * 16, 16), 16)
            dst = pl.ds(pl.multiple_of(dz * SLOTS + n * 16, 16), 16)
            gate, up = pre[src, :FF], pre[src, FF:]
            sig = jax.nn.sigmoid(gate)
            active = gate * sig
            hid[dst, :] = (active * up).astype(BF)
            dgu[dst, :FF] = (up * (sig * (1.0 + gate * (1.0 - sig)))).astype(BF)
            dgu[dst, FF:] = active.astype(BF)

        loop(SLOTS // 16, act)

    def core_wait(table, dz):
        for part in range(3):
            table[dz, part].wait_recv()

    def cot_one(dz):
        z_cot0[dz].wait_recv()
        own_in(cots, core_cot, dz)
        own_on(cots, core_cot, dz)

    def cot_two(dz):
        z_cot1[dz].wait_recv()
        core_cot[dz, 1] = cross(cots, dz, 1, A)
        last_in(cots, core_cot, dz)

    core_wait(core_tok, 0)
    forward_one(0)
    core_wait(core_tok, 1)
    forward_one(1)
    c_cot.wait_recv()
    fill(gates_p, cot_p, cots, 1, 1, True, CA, 896)
    z_cot1 = {dz: spread(cots, 1, 1, dz) for dz in (1, 3, 2)}
    core_cot[0, 1] = cross(cots, 0, 1, A)
    d3 = w_forward(wd, 1 - xh, d1)
    last_in(cots, core_cot, 0)
    core_wait(core_tok, 3)
    forward_one(3)
    core_wait(core_tok, 2)
    forward_one(2)
    for dz in (1, 3, 2):
        cot_one(dz)

    for copy in d2 + d3:
        copy.wait_recv()

    def product(left, right, dz, arr):
        here = pl.ds(dz * SLOTS, SLOTS)

        def tile(n):
            cols = pl.ds(pl.multiple_of(n * 1280, 256), 1280)
            val = dot(left[here, :], right[cols, :], NT).astype(BF)
            pown[pl.ds((arr * 4 + dz) * HALF, HALF), cols] = val[:HALF]
            psend[pl.ds(dz * HALF, HALF), cols] = val[HALF:]

        loop(D // 1280, tile)

    def hand_over(dz):
        part = pl.ds(dz * HALF, HALF)
        return send(psend.at[part], precv.at[part], to_core)

    def add_up(dz, arr, copy):
        copy.wait_recv()

        def tile(n):
            k = pl.multiple_of(n * 16, 16)
            a = pown[pl.ds((arr * 4 + dz) * HALF + k, 16), :].astype(F32)
            b = precv[pl.ds(dz * HALF + k, 16), :].astype(F32)
            pown[pl.ds((arr * 4 + dz) * HALF + k, 16), :] = (a + b).astype(BF)

        loop(HALF // 16, tile)

    def swap(dz, arr):
        src = pown.at[pl.ds((arr * 4 + dz) * HALF + CAP, CAP), B]
        copy = send(src, xret.at[pl.ds((arr * 4 + dz) * CAP, CAP)], to_x)
        late.append(copy)
        swapped[arr, dz] = copy

    def add_swapped(dz, arr):
        swapped[arr, dz].wait_recv()
        a = pown[pl.ds((arr * 4 + dz) * HALF, CAP), CA:].astype(F32)
        b = xret[pl.ds((arr * 4 + dz) * CAP, CAP), :].astype(F32)
        pown[pl.ds((arr * 4 + dz) * HALF, CAP), CA:] = (a + b).astype(BF)

    parts = (pl.ds(0, CA // 2), pl.ds(CA // 2, CA // 2), B)

    def give(dz, arr, n, dx):
        src = pown.at[pl.ds((arr * 4 + dz) * HALF + dx * CAP, CAP), parts[n]]
        dst = ret.at[pl.ds((arr * 2 + dx) * SLOTS + dz * CAP, CAP), parts[n]]
        if dz == 0:
            copy = pltpu.make_async_copy(src, dst, loc_sem.at[13 + arr * 5 + n * 2 + dx])
            copy.start()
        else:
            copy = send(src, dst, at_z(dz))
            late.append(copy)
        back[arr, n, dz, dx] = copy

    def give_back(arr, n):
        for dz in (1, 3, 2, 0):
            give(dz, arr, n, 0)
            give(dz, arr, n, 1)

    def give_last(arr):
        for dz in (1, 3, 2, 0):
            add_swapped(dz, arr)
            give(dz, arr, 2, 0)

    def given(arr, n):
        for dx in (0, 1) if n < 2 else (0,):
            back[arr, n, 0, dx].wait()
            for dz in (1, 3, 2):
                back[arr, n, dz, dx].wait_recv()

    order = (0, 1, 3, 2)
    hand, hand_b = {}, {}
    back, swapped = {}, {}
    for dz in order:
        product(hid, wd, dz, 0)
        hand[dz] = hand_over(dz)
    for dz in order:
        add_up(dz, 0, hand[dz])
        swap(dz, 0)
        pl.semaphore_signal(credit.at[dz], inc=1, device_id=to_core, device_id_type=MESH)

    def backward_one(dz):
        here = pl.ds(dz * SLOTS, SLOTS)
        pre[:, :FF] = dot(cots[here, :], wd[...], NN)

        def act(n):
            src = pl.ds(pl.multiple_of(n * 16, 16), 16)
            dst = pl.ds(pl.multiple_of(dz * SLOTS + n * 16, 16), 16)
            dh = pre[src, :FF]
            dgu[dst, :FF] = (dgu[dst, :FF].astype(F32) * dh).astype(BF)
            dgu[dst, FF:] = (dgu[dst, FF:].astype(F32) * dh).astype(BF)

        loop(SLOTS // 16, act)

    def backward_two(dz):
        hand[dz].wait_send()
        pl.semaphore_wait(credit.at[dz], 1)
        product(dgu, wgu, dz, 1)
        hand_b[dz] = hand_over(dz)

    give_back(0, 0)
    give_back(0, 1)
    for dz in (1, 3, 2):
        cot_two(dz)
    core_wait(core_cot, 0)
    backward_one(0)
    backward_two(0)
    for dz in (1, 3, 2):
        core_wait(core_cot, dz)

    near = y // 2
    other = 1 - xh

    def weight_grad(left, right, buf, xh_, pair):
        at = pl.ds(pl.multiple_of((xh_ * 2 + pair) * 2 * SH, 128), 2 * SH)
        buf[at, :] = dot(left[:, at], right[...], TN).astype(BF)

    def add_into(buf, start, land, k):
        def tile(n):
            r = pl.multiple_of(n * 16, 16)
            at = pl.ds(pl.multiple_of(start + r, 16), 16)
            a = buf[at, :].astype(F32) + land[k, pl.ds(r, 16), :].astype(F32)
            buf[at, :] = a.astype(BF)

        loop(SH // 2 // 16, tile)

    def ring_first(buf, land, k, xh_):
        up = send(shard(buf, xh_, y_far, 0, SH // 2), land.at[k], to_yup)
        dn = send(shard(buf, xh_, y_far, SH // 2, SH // 2), land.at[2 + k], to_ydn)
        late.extend([up, dn])
        return up, dn

    def ring_second(buf, land, land2, k, xh_, pair):
        up, dn = pair
        up.wait_recv()
        add_into(buf, (xh_ * 4 + y_up) * SH, land, k)
        on_up = send(shard(buf, xh_, y_up), land2.at[k], to_yup)
        dn.wait_recv()
        add_into(buf, (xh_ * 4 + y_dn) * SH + SH // 2, land, 2 + k)
        on_dn = send(shard(buf, xh_, y_dn), land2.at[2 + k], to_ydn)
        late.extend([on_up, on_dn])
        return on_up, on_dn

    def owner_value(buf, land, k, xh_):
        start = (xh_ * 4 + y) * SH

        def value(r):
            at = pl.ds(pl.multiple_of(start + r, 16), 16)
            here = pl.ds(r, 16)
            total = buf[at, :].astype(F32) + land[k, here, :].astype(F32)
            return total + land[2 + k, here, :].astype(F32)

        return start, value

    def ring_third(buf, land, recv, pair):
        for copy in pair:
            copy.wait_recv()
        start, value = owner_value(buf, land, 0, other)

        def tile(n):
            r = pl.multiple_of(n * 16, 16)
            buf[pl.ds(pl.multiple_of(start + r, 16), 16), :] = value(r).astype(BF)

        loop(SH // 16, tile)
        copy = send(shard(buf, other, y), recv, to_xh)
        late.append(copy)
        return copy

    def ring_last(buf, land, recv, out, pair, copy):
        for c_ in pair:
            c_.wait_recv()
        copy.wait_recv()
        _, value = owner_value(buf, land, 1, xh)

        def tile(n):
            r = pl.multiple_of(n * 16, 16)
            out[pl.ds(r, 16), :] = value(r) + recv[pl.ds(r, 16), :].astype(F32)

        loop(SH // 16, tile)

    def pick(mat_ref, arr):
        mat = mat_ref[...]
        return jnp.where(mat > 0, jnp.ones_like(mat), jnp.zeros_like(mat)) if arr else mat

    fins = {}

    def combine(arr, n):
        given(arr, n)
        held = (tok_p, cot_p)[arr]
        part = ret[pl.ds((arr * 2 + 1) * SLOTS, SLOTS), parts[n]]
        held[:, parts[n]] = dot(pick(gates_p, arr), part, TN).astype(BF)
        copy = send(held.at[:, parts[n]], fin_recv.at[arr, :, parts[n]], to_x)
        late.append(copy)
        fins[arr, n] = copy

    def finish(arr, n, dst):
        if n == 2:
            given(arr, n)
        part = ret[pl.ds(arr * 2 * SLOTS, SLOTS), parts[n]]
        total = dot(pick(gates, arr), part, TN)
        if n < 2:
            fins[arr, n].wait_recv()
            total = total + fin_recv[arr, :, parts[n]].astype(F32)
        dst[:, parts[n]] = total.astype(BF)

    def settle(dz):
        add_up(dz, 1, hand_b[dz])
        swap(dz, 1)

    weight_grad(cots, hid, gd, other, 1 - near)
    d_a = ring_first(gd, y1d, 0, other)
    weight_grad(cots, hid, gd, xh, 1 - near)
    d_b = ring_first(gd, y1d, 1, xh)
    weight_grad(cots, hid, gd, other, near)
    weight_grad(cots, hid, gd, xh, near)
    settle(0)
    backward_one(1)
    backward_two(1)
    d_a = ring_second(gd, y1d, y2d, 0, other, d_a)
    d_b = ring_second(gd, y1d, y2d, 1, xh, d_b)
    backward_one(3)
    settle(1)
    backward_two(3)
    give_last(0)
    backward_one(2)
    settle(3)
    weight_grad(rows, dgu, ggu, other, 1 - near)
    gu_a = ring_first(ggu, y1gu, 0, other)
    backward_two(2)
    weight_grad(rows, dgu, ggu, other, near)
    settle(2)
    give_back(1, 0)
    weight_grad(rows, dgu, ggu, xh, 1 - near)
    gu_b = ring_first(ggu, y1gu, 1, xh)
    gu_a = ring_second(ggu, y1gu, y2gu, 0, other, gu_a)
    d_x = ring_third(gd, y2d, xd, d_a)
    weight_grad(rows, dgu, ggu, xh, near)
    c_tok.wait_send()
    c_cot.wait_send()
    combine(0, 0)
    combine(0, 1)
    give_back(1, 1)
    give_last(1)
    finish(0, 2, out_ref)
    gu_b = ring_second(ggu, y1gu, y2gu, 1, xh, gu_b)
    ring_last(gd, y2d, xd, gd_ref, d_b, d_x)
    finish(0, 0, out_ref)
    finish(0, 1, out_ref)
    gu_x = ring_third(ggu, y2gu, xgu, gu_a)
    combine(1, 0)
    combine(1, 1)
    finish(1, 2, tgrad_ref)
    finish(1, 0, tgrad_ref)
    ring_last(ggu, y2gu, xgu, ggu_ref, gu_b, gu_x)
    finish(1, 1, tgrad_ref)

    for copy in late:
        copy.wait_send()
    for dz in order:
        hand_b[dz].wait_send()
    assert used[0] <= N_COPY, used[0]


N_COPY = 200


def exchange(ids, gates, tok, cot, proj_in, proj_out):
    vmem = pl.BlockSpec(memory_space=pltpu.VMEM)
    hbm = pl.BlockSpec(memory_space=pl.ANY)
    shapes = [
        jax.ShapeDtypeStruct((TOK, D), BF),
        jax.ShapeDtypeStruct((TOK, D), BF),
        jax.ShapeDtypeStruct((SH, 2 * FF), F32),
        jax.ShapeDtypeStruct((SH, FF), F32),
    ]
    scratch = [
        pltpu.VMEM((SLOTS, TOK), BF),
        pltpu.VMEM((SLOTS, TOK), BF),
        pltpu.VMEM((TOK, CA), BF),
        pltpu.VMEM((TOK, CA), BF),
        pltpu.VMEM((6 * CAP, D), BF),
        pltpu.VMEM((6 * CAP, CA), BF),
        pltpu.VMEM((ROWS, D), BF),
        pltpu.VMEM((ROWS, D), BF),
        pltpu.VMEM((D, 2 * FF), BF),
        pltpu.VMEM((D, FF), BF),
        pltpu.VMEM((ROWS, FF), BF),
        pltpu.VMEM((ROWS, 2 * FF), BF),
        pltpu.VMEM((4 * HALF, D), BF),
        pltpu.VMEM((8 * HALF, D), BF),
        pltpu.VMEM((4 * HALF, D), BF),
        pltpu.VMEM((4 * SLOTS, D), BF),
        pltpu.VMEM((2, TOK, CA), BF),
        pltpu.VMEM((2 * SLOTS, CB), BF),
        pltpu.VMEM((D, 2 * FF), BF),
        pltpu.VMEM((D, FF), BF),
        pltpu.VMEM((4, SH // 2, 2 * FF), BF),
        pltpu.VMEM((4, SH // 2, FF), BF),
        pltpu.VMEM((4, SH, 2 * FF), BF),
        pltpu.VMEM((4, SH, FF), BF),
        pltpu.VMEM((SH, 2 * FF), BF),
        pltpu.VMEM((SH, FF), BF),
        pltpu.SemaphoreType.DMA((N_COPY,)),
        pltpu.SemaphoreType.DMA((N_COPY,)),
        pltpu.SemaphoreType.DMA((23,)),
        pltpu.SemaphoreType.REGULAR((4,)),
    ]
    return pl.pallas_call(
        kernel,
        out_shape=shapes,
        in_specs=[vmem] * 2 + [hbm] * 4,
        out_specs=[vmem] * 4,
        scratch_shapes=scratch,
        compiler_params=pltpu.CompilerParams(
            collective_id=0, has_side_effects=True, vmem_limit_bytes=64 * 2**20
        ),
        cost_estimate=pl.CostEstimate(
            flops=18 * ROWS * D * FF, bytes_accessed=2**22, transcendentals=ROWS * FF
        ),
        name="experts",
    )(ids, gates, tok, cot, proj_in, proj_out)


def adam_kernel(ggu, gd, pin, pout, first, second, out, tgrad, *outs):
    new_in, new_out, new_first, new_second, out_copy, tgrad_copy = outs
    out_copy[...] = out[...]
    tgrad_copy[...] = tgrad[...]
    for k in range(3):
        gradient = gd[...] if k == 2 else ggu[:, k * FF : (k + 1) * FF]
        master = pout[0] if k == 2 else pin[k, 0]
        m = beta_one * first[k, 0] + (1.0 - beta_one) * gradient
        v = beta_two * second[k, 0] + (1.0 - beta_two) * gradient * gradient
        step = m / bias_one / (jnp.sqrt(v / bias_two) + adam_eps) + decay_rate * master
        updated = master - learn_rate * step
        new_first[k, 0] = m
        new_second[k, 0] = v
        if k == 2:
            new_out[0] = updated
        else:
            new_in[k, 0] = updated


def adam(ggu, gd, pin, pout, first, second, out, tgrad):
    steps = 4
    part = SH // steps

    def stacked(count):
        return pl.BlockSpec((count, 1, part, FF), lambda i: (0, 0, i, 0))

    plain = [
        pl.BlockSpec((part, 2 * FF), lambda i: (i, 0)),
        pl.BlockSpec((part, FF), lambda i: (i, 0)),
    ]
    single = pl.BlockSpec((1, part, FF), lambda i: (0, i, 0))
    token = pl.BlockSpec((TOK // steps, D), lambda i: (i, 0))
    arrays = (pin, pout, first, second, out, tgrad)
    specs = [stacked(2), single, stacked(3), stacked(3), token, token]
    return pl.pallas_call(
        adam_kernel,
        out_shape=[jax.ShapeDtypeStruct(a.shape, a.dtype) for a in arrays],
        grid=(steps,),
        in_specs=plain + specs,
        out_specs=specs,
        compiler_params=pltpu.CompilerParams(vmem_limit_bytes=64 * 2**20),
        name="adam",
    )(ggu, gd, *arrays)


def per_device(
    tokens, route_ids, route_gates, out_grad, proj_in, proj_out, first_moment, second_moment
):
    layer_out, token_grad, ggu, gd = exchange(
        route_ids.T, route_gates.T, tokens, out_grad, proj_in, proj_out
    )
    new_in, new_out, new_first, new_second, layer_out, token_grad = adam(
        ggu, gd, proj_in, proj_out, first_moment, second_moment, layer_out, token_grad
    )
    return (layer_out, token_grad, new_in, new_out, new_first, new_second)


def solution(mesh):
    rows = P(("group", "member"), None)
    return jax.shard_map(
        per_device,
        mesh=mesh,
        in_specs=(
            rows,
            rows,
            rows,
            rows,
            P(None, "member", "group", None),
            P("member", "group", None),
            P(None, "member", "group", None),
            P(None, "member", "group", None),
        ),
        out_specs=(
            rows,
            rows,
            P(None, "member", "group", None),
            P("member", "group", None),
            P(None, "member", "group", None),
            P(None, "member", "group", None),
        ),
        check_vma=False,
    )
```

```python
import functools

import jax
import jax.numpy as jnp
from jax import lax
from jax.experimental import pallas as pl
from jax.experimental.pallas import tpu as pltpu
from jax.sharding import PartitionSpec as P

MESH = pl.DeviceIdType.MESH
BF = jnp.bfloat16
F32 = jnp.float32
CAP = 80
WIN = 4
TOK = 128
D = 2560
FF = 384
SH = 320
SLOTS = WIN * CAP
ROWS = 16 * CAP
HALF = 2 * CAP
CA = 1792
CC = 1536
CF = 1536
CG = 1792

beta_one = 0.9
beta_two = 0.95
learn_rate = 0.0003
decay_rate = 0.1
adam_eps = 1e-08
bias_one = 1.0 - 0.9**10
bias_two = 1.0 - 0.95**10

NN = (((1,), (0,)), ((), ()))
NT = (((1,), (1,)), ((), ()))
TN = (((0,), (0,)), ((), ()))


def dot(a, b, dims):
    return lax.dot_general(a, b, dims, preferred_element_type=F32)


def loop(count, body):
    lax.fori_loop(0, count, lambda i, c: (body(i), c)[1], 0)


def slot_table(z, ids_ref, gate_ref, table):
    ids = ids_ref[...]
    value = gate_ref[...].astype(F32)
    down = lax.broadcasted_iota(jnp.int32, (TOK, TOK), 0)
    lane = lax.broadcasted_iota(jnp.int32, (TOK, TOK), 1)
    row = lax.broadcasted_iota(jnp.int32, (8, TOK), 0)
    named = jnp.zeros((8, TOK), F32)
    match, weight = [], []
    for dz in range(WIN):
        hit = ids == (z - dz + WIN) % WIN
        match.append(jnp.sum(jnp.where(hit, 1.0, 0.0), axis=0, keepdims=True))
        weight.append(jnp.sum(jnp.where(hit, value, 0.0), axis=0, keepdims=True))
        named = jnp.where(row == dz, match[dz], named)
    upto = jnp.where(down <= lane, 1.0, 0.0).astype(BF)
    count = dot(named.astype(BF), upto, NN)
    for dz in range(WIN):
        table[dz : dz + 1, :] = jnp.where(match[dz] > 0, count[dz : dz + 1] - 1.0, -1.0)
        table[WIN + dz : WIN + dz + 1, :] = weight[dz]


def slot_gates(table, gates):
    slot = lax.broadcasted_iota(jnp.int32, (CAP, TOK), 0)
    for dz in range(WIN):
        place = table[dz : dz + 1, :].astype(jnp.int32)
        gate = jnp.where(slot == place, table[WIN + dz : WIN + dz + 1, :], 0.0)
        gates[pl.ds(dz * CAP, CAP), :] = gate.astype(BF)


def kernel(
    ids_ref,
    gate_ref,
    tok_hbm,
    cot_hbm,
    proj_in,
    proj_out,
    out_hbm,
    tgrad_hbm,
    ggu_hbm,
    gd_hbm,
    out_ref,
    tgrad_ref,
    ggu_ref,
    gd_ref,
    table,
    table_p,
    gates,
    gates_p,
    tok_p,
    cot_p,
    slots,
    slots_p,
    rows,
    cots,
    wgu,
    wd,
    hid,
    dgu,
    psend,
    pown,
    precv,
    ret,
    fin_recv0,
    fin_recv1,
    xret0,
    xret1,
    ggu,
    gd,
    y1gu,
    y1d,
    y2gu,
    y2d,
    xgu,
    xd,
    send_sem,
    recv_sem,
    loc_sem,
    credit,
):
    tok, cot, pre = out_ref, tgrad_ref, ggu_ref
    g = lax.axis_index("group")
    m = lax.axis_index("member")
    xh, y = g // 4, g % 4
    z, xc = m // 4, m % 4
    x, c = xc // 2, xc % 2
    to_core = (g, z * 4 + x * 2 + (1 - c))
    to_x = (g, z * 4 + (1 - x) * 2 + c)

    def at_z(step):
        return (g, ((z + step) % 4) * 4 + xc)

    y_up, y_dn, y_far = (y + 1) % 4, (y + 3) % 4, (y + 2) % 4
    to_yup = (xh * 4 + y_up, m)
    to_ydn = (xh * 4 + y_dn, m)
    to_xh = ((1 - xh) * 4 + y, m)

    used = [0, 0]
    free = []
    which = {}

    def send(src, dst, target):
        i = used[0]
        used[0] += 1
        if free:
            k = free.pop()
        else:
            k = used[1]
            used[1] += 1
        copy = pltpu.make_async_remote_copy(
            src_ref=src,
            dst_ref=dst,
            send_sem=send_sem.at[k],
            recv_sem=recv_sem.at[i],
            device_id=target,
            device_id_type=MESH,
        )
        copy.start()
        which[id(copy)] = k
        return copy

    loads = [
        pltpu.make_async_copy(tok_hbm, tok, loc_sem.at[8]),
        pltpu.make_async_copy(proj_in.at[0, 0], pre.at[:, pl.ds(0, FF)], loc_sem.at[9]),
        pltpu.make_async_copy(proj_in.at[1, 0], pre.at[:, pl.ds(FF, FF)], loc_sem.at[10]),
        pltpu.make_async_copy(proj_out.at[0], gd_ref, loc_sem.at[11]),
        pltpu.make_async_copy(cot_hbm, cot, loc_sem.at[12]),
    ]
    for copy in loads:
        copy.start()
    barrier = pltpu.get_barrier_semaphore()
    for other in (to_core, to_x, at_z(1), at_z(2), at_z(3), to_yup, to_ydn, to_xh):
        pl.semaphore_signal(barrier, inc=1, device_id=other, device_id_type=MESH)
    slot_table(z, ids_ref, gate_ref, table)
    slot_gates(table, gates)
    for copy in loads[:4]:
        copy.wait()
    own = pl.ds(pl.multiple_of((xh * 4 + y) * SH, SH), SH)
    wgu[own, :] = pre[...].astype(BF)
    wd[own, :] = gd_ref[...].astype(BF)
    pl.semaphore_wait(barrier, 8)

    def shard(ref, xh_, y_, first=0, count=SH):
        start = pl.multiple_of((xh_ * 4 + y_) * SH + first, 16)
        return ref.at[pl.ds(start, count)]

    def block(ref, dz, dc, dx):
        return ref.at[pl.ds(dz * SLOTS + dc * HALF + dx * CAP, CAP)]

    late = []

    c_gates = send(table, table_p, to_x)
    late.append(c_gates)

    def w_first(buf):
        part = shard(buf, xh, y)
        up = send(part, part, to_yup)
        dn = send(part, part, to_ydn)
        late.extend([up, dn])
        return up, dn

    def w_far(buf):
        far = send(shard(buf, xh, y), shard(buf, xh, y), to_xh)
        late.append(far)
        return far

    def w_second(buf, far):
        far.wait_recv()
        part = shard(buf, 1 - xh, y)
        up = send(part, part, to_yup)
        dn = send(part, part, to_ydn)
        late.extend([up, dn])
        return up, dn

    def w_forward(buf, xh_, pair):
        up, dn = pair
        up.wait_recv()
        part = shard(buf, xh_, y_dn, 0, SH // 2)
        on_up = send(part, part, to_yup)
        dn.wait_recv()
        part = shard(buf, xh_, y_up, SH // 2, SH // 2)
        on_dn = send(part, part, to_ydn)
        late.extend([on_up, on_dn])
        return on_up, on_dn

    gu0 = w_first(wgu)
    gu_far = w_far(wgu)

    def fill(mat_ref, val_ref, dst, dx, base, gated, width, step):
        held = (slots, slots_p)[dx]
        mat = mat_ref[...]
        if not gated:
            mat = jnp.where(mat > 0, jnp.ones_like(mat), jnp.zeros_like(mat))

        def tile(n):
            cols = pl.ds(pl.multiple_of(n * step, 128), step)
            val = dot(mat, val_ref[:, cols], NN).astype(BF)
            dst[pl.ds(dx * CAP, CAP), cols] = val[:CAP]
            held[pl.ds(base * 3 * CAP, 3 * CAP), cols] = val[CAP:]

        loop(width // step, tile)

    def x_first(dst):
        return pl.ds(0, CA if dst is rows else CC)

    def z_first(dst):
        return pl.ds(CA, D - CA) if dst is rows else pl.ds(CC, D - CC)

    def spread(dst, dx, base, dz):
        src = (slots, slots_p)[dx].at[pl.ds((base * 3 + dz - 1) * CAP, CAP)]
        land = block(dst, dz, 0, dx)
        if dx == 1:
            cols = x_first(dst)
            src, land = src.at[:, cols], land.at[:, cols]
        copy = send(src, land, at_z(4 - dz))
        late.append(copy)
        return copy

    def cross(dst, dz, dx, cols):
        copy = send(
            block(dst, dz, 0, dx).at[:, cols], block(dst, dz, 1, dx).at[:, cols], to_core
        )
        late.append(copy)
        return copy

    def own_in(dst, table, dz):
        table[dz, 0] = cross(dst, dz, 0, pl.ds(0, D))

    def own_on(dst, table, dz):
        cols = z_first(dst)
        copy = send(block(dst, dz, 0, 0).at[:, cols], block(dst, dz, 0, 1).at[:, cols], to_x)
        late.append(copy)
        table[dz, "x"] = copy

    def last_in(dst, table, dz):
        table[dz, "x"].wait_recv()
        table[dz, 2] = cross(dst, dz, 1, z_first(dst))

    core_tok, core_cot = {}, {}
    fill(gates, tok, rows, 0, 0, False, D, 512)
    z_tok0 = {dz: spread(rows, 0, 0, dz) for dz in (1, 3, 2)}
    own_in(rows, core_tok, 0)
    c_tok = send(tok.at[:, x_first(rows)], tok_p, to_x)
    loads[4].wait()
    fill(gates, cot, cots, 0, 1, True, D, 512)
    gu2 = w_forward(wgu, xh, gu0)
    gu1 = w_second(wgu, gu_far)
    for dz in (1, 3, 2):
        z_tok0[dz].wait_recv()
        own_in(rows, core_tok, dz)
    z_cot0 = {2: spread(cots, 0, 1, 2)}
    c_gates.wait_recv()
    slot_gates(table_p, gates_p)
    c_tok.wait_recv()
    for dz in (0, 1, 3, 2):
        own_on(rows, core_tok, dz)
    fill(gates_p, tok_p, rows, 1, 0, False, CA, 896)
    z_tok1 = {dz: spread(rows, 1, 0, dz) for dz in (1, 3, 2)}
    core_tok[0, 1] = cross(rows, 0, 1, x_first(rows))
    d0 = w_first(wd)
    d_far = w_far(wd)
    gu3 = w_forward(wgu, 1 - xh, gu1)
    c_cot = send(cot.at[:, x_first(cots)], cot_p, to_x)
    z_cot0[1] = spread(cots, 0, 1, 1)
    z_cot0[3] = spread(cots, 0, 1, 3)
    d2 = w_forward(wd, xh, d0)
    d1 = w_second(wd, d_far)
    last_in(rows, core_tok, 0)
    own_in(cots, core_cot, 0)
    own_on(cots, core_cot, 0)
    for dz in (1, 3, 2):
        z_tok1[dz].wait_recv()
        core_tok[dz, 1] = cross(rows, dz, 1, x_first(rows))
    for dz in (1, 3, 2):
        last_in(rows, core_tok, dz)

    for copy in gu2 + gu3:
        copy.wait_recv()

    def forward_one(dz):
        here = pl.ds(dz * SLOTS, SLOTS)

        pre[...] = dot(rows[here, :], wgu[...], NN)

        def act(n):
            src = pl.ds(pl.multiple_of(n * 16, 16), 16)
            dst = pl.ds(pl.multiple_of(dz * SLOTS + n * 16, 16), 16)
            gate, up = pre[src, :FF], pre[src, FF:]
            sig = jax.nn.sigmoid(gate)
            active = gate * sig
            hid[dst, :] = (active * up).astype(BF)
            dgu[dst, :FF] = (up * (sig * (1.0 + gate * (1.0 - sig)))).astype(BF)
            dgu[dst, FF:] = active.astype(BF)

        loop(SLOTS // 16, act)

    def core_wait(table, dz):
        for part in range(3):
            table[dz, part].wait_recv()

    def cot_one(dz):
        z_cot0[dz].wait_recv()
        own_in(cots, core_cot, dz)
        own_on(cots, core_cot, dz)

    def cot_two(dz):
        z_cot1[dz].wait_recv()
        core_cot[dz, 1] = cross(cots, dz, 1, x_first(cots))
        last_in(cots, core_cot, dz)

    core_wait(core_tok, 0)
    forward_one(0)
    c_cot.wait_recv()
    fill(gates_p, cot_p, cots, 1, 1, True, CC, 768)
    z_cot1 = {dz: spread(cots, 1, 1, dz) for dz in (1, 3, 2)}
    core_cot[0, 1] = cross(cots, 0, 1, x_first(cots))
    core_wait(core_tok, 1)
    forward_one(1)
    d3 = w_forward(wd, 1 - xh, d1)
    last_in(cots, core_cot, 0)
    core_wait(core_tok, 3)
    forward_one(3)
    for dz in (1, 3, 2):
        cot_one(dz)
    core_wait(core_tok, 2)
    forward_one(2)

    for copy in d2 + d3:
        copy.wait_recv()

    def product(left, right, dz, arr):
        here = pl.ds(dz * SLOTS, SLOTS)

        def tile(n):
            cols = pl.ds(pl.multiple_of(n * 1280, 256), 1280)
            val = dot(left[here, :], right[cols, :], NT).astype(BF)
            pown[pl.ds((arr * 4 + dz) * HALF, HALF), cols] = val[:HALF]
            psend[pl.ds(dz * HALF, HALF), cols] = val[HALF:]

        loop(D // 1280, tile)

    def hand_over(dz):
        part = pl.ds(dz * HALF, HALF)
        return send(psend.at[part], precv.at[part], to_core)

    def add_up(dz, arr, copy):
        copy.wait_recv()

        def tile(n):
            k = pl.multiple_of(n * 16, 16)
            a = pown[pl.ds((arr * 4 + dz) * HALF + k, 16), :].astype(F32)
            b = precv[pl.ds(dz * HALF + k, 16), :].astype(F32)
            pown[pl.ds((arr * 4 + dz) * HALF + k, 16), :] = (a + b).astype(BF)

        loop(HALF // 16, tile)

    parts = [
        (pl.ds(0, n // 2), pl.ds(n // 2, n // 2), pl.ds(n, D - n)) for n in (CF, CG)
    ]
    xrets = (xret0, xret1)

    def swap(dz, arr):
        src = pown.at[pl.ds((arr * 4 + dz) * HALF + CAP, CAP), parts[arr][2]]
        copy = send(src, xrets[arr].at[pl.ds(dz * CAP, CAP)], to_x)
        late.append(copy)
        swapped[arr, dz] = copy

    def add_swapped(dz, arr):
        swapped[arr, dz].wait_recv()
        cols = parts[arr][2]
        a = pown[pl.ds((arr * 4 + dz) * HALF, CAP), cols].astype(F32)
        b = xrets[arr][pl.ds(dz * CAP, CAP), :].astype(F32)
        pown[pl.ds((arr * 4 + dz) * HALF, CAP), cols] = (a + b).astype(BF)

    def give(dz, arr, n, dx):
        src = pown.at[pl.ds((arr * 4 + dz) * HALF + dx * CAP, CAP), parts[arr][n]]
        dst = ret.at[pl.ds((arr * 2 + dx) * SLOTS + dz * CAP, CAP), parts[arr][n]]
        if dz == 0:
            copy = pltpu.make_async_copy(src, dst, loc_sem.at[13 + arr * 5 + n * 2 + dx])
            copy.start()
        else:
            copy = send(src, dst, at_z(dz))
            late.append(copy)
        back[arr, n, dz, dx] = copy

    def give_back(arr, n):
        for dz in (1, 3, 2, 0):
            give(dz, arr, n, 0)
            give(dz, arr, n, 1)

    def give_last(arr):
        for dz in (1, 3, 2, 0):
            add_swapped(dz, arr)
            give(dz, arr, 2, 0)

    def given(arr, n):
        for dx in (0, 1) if n < 2 else (0,):
            back[arr, n, 0, dx].wait()
            for dz in (1, 3, 2):
                back[arr, n, dz, dx].wait_recv()

    order = (0, 1, 3, 2)
    hand, hand_b = {}, {}
    back, swapped = {}, {}
    for dz in order:
        product(hid, wd, dz, 0)
        hand[dz] = hand_over(dz)
    for dz in order:
        add_up(dz, 0, hand[dz])
        pl.semaphore_signal(credit.at[dz], inc=1, device_id=to_core, device_id_type=MESH)

    def backward_one(dz):
        here = pl.ds(dz * SLOTS, SLOTS)
        pre[:, :FF] = dot(cots[here, :], wd[...], NN)

        def act(n):
            src = pl.ds(pl.multiple_of(n * 16, 16), 16)
            dst = pl.ds(pl.multiple_of(dz * SLOTS + n * 16, 16), 16)
            dh = pre[src, :FF]
            dgu[dst, :FF] = (dgu[dst, :FF].astype(F32) * dh).astype(BF)
            dgu[dst, FF:] = (dgu[dst, FF:].astype(F32) * dh).astype(BF)

        loop(SLOTS // 16, act)

    def backward_two(dz):
        hand[dz].wait_send()
        pl.semaphore_wait(credit.at[dz], 1)
        product(dgu, wgu, dz, 1)
        hand_b[dz] = hand_over(dz)

    early = len(late)
    give_back(0, 0)
    cot_two(1)
    core_wait(core_cot, 0)
    backward_one(0)
    cot_two(3)
    backward_two(0)
    cot_two(2)
    for dz in (1, 3, 2):
        core_wait(core_cot, dz)
    give_back(0, 1)
    for dz in order:
        swap(dz, 0)

    near = y // 2
    other = 1 - xh

    def weight_grad(left, right, buf, xh_, pair):
        at = pl.ds(pl.multiple_of((xh_ * 2 + pair) * 2 * SH, 128), 2 * SH)
        buf[at, :] = dot(left[:, at], right[...], TN).astype(BF)

    def add_into(buf, start, land, k):
        def tile(n):
            r = pl.multiple_of(n * 16, 16)
            at = pl.ds(pl.multiple_of(start + r, 16), 16)
            a = buf[at, :].astype(F32) + land[k, pl.ds(r, 16), :].astype(F32)
            buf[at, :] = a.astype(BF)

        loop(SH // 2 // 16, tile)

    def ring_first(buf, land, k, xh_):
        up = send(shard(buf, xh_, y_far, 0, SH // 2), land.at[k], to_yup)
        dn = send(shard(buf, xh_, y_far, SH // 2, SH // 2), land.at[2 + k], to_ydn)
        late.extend([up, dn])
        return up, dn

    def ring_second(buf, land, land2, k, xh_, pair):
        up, dn = pair
        up.wait_recv()
        add_into(buf, (xh_ * 4 + y_up) * SH, land, k)
        on_up = send(shard(buf, xh_, y_up), land2.at[k], to_yup)
        dn.wait_recv()
        add_into(buf, (xh_ * 4 + y_dn) * SH + SH // 2, land, 2 + k)
        on_dn = send(shard(buf, xh_, y_dn), land2.at[2 + k], to_ydn)
        late.extend([on_up, on_dn])
        return on_up, on_dn

    def owner_value(buf, land, k, xh_):
        start = (xh_ * 4 + y) * SH

        def value(r):
            at = pl.ds(pl.multiple_of(start + r, 16), 16)
            here = pl.ds(r, 16)
            total = buf[at, :].astype(F32) + land[k, here, :].astype(F32)
            return total + land[2 + k, here, :].astype(F32)

        return start, value

    def ring_third(buf, land, recv, pair):
        for copy in pair:
            copy.wait_recv()
        start, value = owner_value(buf, land, 0, other)

        def tile(n):
            r = pl.multiple_of(n * 16, 16)
            buf[pl.ds(pl.multiple_of(start + r, 16), 16), :] = value(r).astype(BF)

        loop(SH // 16, tile)
        copy = send(shard(buf, other, y), recv, to_xh)
        late.append(copy)
        return copy

    def ring_last(buf, land, recv, out, pair, copy):
        for c_ in pair:
            c_.wait_recv()
        copy.wait_recv()
        _, value = owner_value(buf, land, 1, xh)

        def tile(n):
            r = pl.multiple_of(n * 16, 16)
            out[pl.ds(r, 16), :] = value(r) + recv[pl.ds(r, 16), :].astype(F32)

        loop(SH // 16, tile)

    def pick(mat_ref, arr):
        mat = mat_ref[...]
        return jnp.where(mat > 0, jnp.ones_like(mat), jnp.zeros_like(mat)) if arr else mat

    fins = {}
    fin_recv = (fin_recv0, fin_recv1)

    def combine(arr, n):
        given(arr, n)
        held = (cot_p, tok_p)[arr]
        part = ret[pl.ds((arr * 2 + 1) * SLOTS, SLOTS), parts[arr][n]]
        held[:, parts[arr][n]] = dot(pick(gates_p, arr), part, TN).astype(BF)
        copy = send(held.at[:, parts[arr][n]], fin_recv[arr].at[:, parts[arr][n]], to_x)
        late.append(copy)
        fins[arr, n] = copy

    def finish(arr, n, dst):
        if n == 2:
            given(arr, n)
        part = ret[pl.ds(arr * 2 * SLOTS, SLOTS), parts[arr][n]]
        total = dot(pick(gates, arr), part, TN)
        if n < 2:
            fins[arr, n].wait_recv()
            total = total + fin_recv[arr][:, parts[arr][n]].astype(F32)
        dst[:, parts[arr][n]] = total.astype(BF)

    def flush():
        for copy in late[:early]:
            copy.wait_send()
            free.append(which[id(copy)])
        del late[:early]

    def settle(dz):
        add_up(dz, 1, hand_b[dz])
        swap(dz, 1)

    weight_grad(cots, hid, gd, other, 1 - near)
    d_a = ring_first(gd, y1d, 0, other)
    weight_grad(cots, hid, gd, other, near)
    flush()
    for dz in (1, 3, 2):
        backward_one(dz)
    d_a = ring_second(gd, y1d, y2d, 0, other, d_a)
    weight_grad(rows, dgu, ggu, other, 1 - near)
    gu_a = ring_first(ggu, y1gu, 0, other)
    weight_grad(rows, dgu, ggu, other, near)
    settle(0)
    backward_two(1)
    backward_two(3)
    settle(1)
    backward_two(2)
    settle(3)
    gu_a = ring_second(ggu, y1gu, y2gu, 0, other, gu_a)
    give_last(0)
    settle(2)
    give_back(1, 0)
    weight_grad(cots, hid, gd, xh, 1 - near)
    d_b = ring_first(gd, y1d, 1, xh)
    weight_grad(cots, hid, gd, xh, near)
    weight_grad(rows, dgu, ggu, xh, 1 - near)
    c_tok.wait_send()
    c_cot.wait_send()
    combine(0, 0)
    combine(0, 1)
    gu_b = ring_first(ggu, y1gu, 1, xh)
    d_x = ring_third(gd, y2d, xd, d_a)
    weight_grad(rows, dgu, ggu, xh, near)
    give_back(1, 1)
    gu_x = ring_third(ggu, y2gu, xgu, gu_a)
    d_b = ring_second(gd, y1d, y2d, 1, xh, d_b)
    gu_b = ring_second(ggu, y1gu, y2gu, 1, xh, gu_b)
    give_last(1)
    finish(0, 2, out_ref)
    stores = []

    def store(src, dst):
        copy = pltpu.make_async_copy(src, dst, loc_sem.at[23 + len(stores)])
        copy.start()
        stores.append(copy)

    ring_last(gd, y2d, xd, gd_ref, d_b, d_x)
    store(gd_ref, gd_hbm)
    finish(0, 0, out_ref)
    finish(0, 1, out_ref)
    store(out_ref, out_hbm)
    combine(1, 0)
    combine(1, 1)
    finish(1, 0, tgrad_ref)
    store(tgrad_ref.at[:, parts[1][0]], tgrad_hbm.at[:, parts[1][0]])
    ring_last(ggu, y2gu, xgu, ggu_ref, gu_b, gu_x)
    store(ggu_ref, ggu_hbm)
    finish(1, 2, tgrad_ref)
    store(tgrad_ref.at[:, parts[1][2]], tgrad_hbm.at[:, parts[1][2]])
    finish(1, 1, tgrad_ref)
    store(tgrad_ref.at[:, parts[1][1]], tgrad_hbm.at[:, parts[1][1]])
    for copy in stores:
        copy.wait()

    for copy in late:
        copy.wait_send()
    for dz in order:
        hand_b[dz].wait_send()
    assert used == [N_COPY, N_SEND], used


N_COPY, N_SEND = 133, 88


def exchange(ids, gates, tok, cot, proj_in, proj_out):
    vmem = pl.BlockSpec(memory_space=pltpu.VMEM)
    hbm = pl.BlockSpec(memory_space=pl.ANY)
    shapes = [
        jax.ShapeDtypeStruct((TOK, D), BF),
        jax.ShapeDtypeStruct((TOK, D), BF),
        jax.ShapeDtypeStruct((SH, 2 * FF), F32),
        jax.ShapeDtypeStruct((SH, FF), F32),
    ]
    scratch = [
        pltpu.VMEM((TOK, D), BF),
        pltpu.VMEM((TOK, D), BF),
        pltpu.VMEM((SH, 2 * FF), F32),
        pltpu.VMEM((SH, FF), F32),
        pltpu.VMEM((2 * WIN, TOK), F32),
        pltpu.VMEM((2 * WIN, TOK), F32),
        pltpu.VMEM((SLOTS, TOK), BF),
        pltpu.VMEM((SLOTS, TOK), BF),
        pltpu.VMEM((TOK, CA), BF),
        pltpu.VMEM((TOK, CC), BF),
        pltpu.VMEM((6 * CAP, D), BF),
        pltpu.VMEM((6 * CAP, CA), BF),
        pltpu.VMEM((ROWS, D), BF),
        pltpu.VMEM((ROWS, D), BF),
        pltpu.VMEM((D, 2 * FF), BF),
        pltpu.VMEM((D, FF), BF),
        pltpu.VMEM((ROWS, FF), BF),
        pltpu.VMEM((ROWS, 2 * FF), BF),
        pltpu.VMEM((4 * HALF, D), BF),
        pltpu.VMEM((8 * HALF, D), BF),
        pltpu.VMEM((4 * HALF, D), BF),
        pltpu.VMEM((4 * SLOTS, D), BF),
        pltpu.VMEM((TOK, CF), BF),
        pltpu.VMEM((TOK, CG), BF),
        pltpu.VMEM((SLOTS, D - CF), BF),
        pltpu.VMEM((SLOTS, D - CG), BF),
        pltpu.VMEM((D, 2 * FF), BF),
        pltpu.VMEM((D, FF), BF),
        pltpu.VMEM((4, SH // 2, 2 * FF), BF),
        pltpu.VMEM((4, SH // 2, FF), BF),
        pltpu.VMEM((4, SH, 2 * FF), BF),
        pltpu.VMEM((4, SH, FF), BF),
        pltpu.VMEM((SH, 2 * FF), BF),
        pltpu.VMEM((SH, FF), BF),
        pltpu.SemaphoreType.DMA((N_SEND,)),
        pltpu.SemaphoreType.DMA((N_COPY,)),
        pltpu.SemaphoreType.DMA((29,)),
        pltpu.SemaphoreType.REGULAR((4,)),
    ]
    return pl.pallas_call(
        kernel,
        out_shape=shapes,
        in_specs=[vmem] * 2 + [hbm] * 4,
        out_specs=[hbm] * 4,
        scratch_shapes=scratch,
        compiler_params=pltpu.CompilerParams(
            collective_id=0, has_side_effects=True, vmem_limit_bytes=64 * 2**20
        ),
        cost_estimate=pl.CostEstimate(
            flops=18 * ROWS * D * FF, bytes_accessed=2**22, transcendentals=ROWS * FF
        ),
        name="experts",
    )(ids, gates, tok, cot, proj_in, proj_out)


def adam_kernel(*refs):
    ggu, gd, pin, pout, first, second, out, tgrad = refs[:8]
    new_in, new_out, new_first, new_second, out_copy, tgrad_copy = refs[8:14]
    grads, masters, firsts, seconds, held, sem = refs[14:]
    passed = [
        pltpu.make_async_copy(out, held.at[0], sem.at[24]),
        pltpu.make_async_copy(tgrad, held.at[1], sem.at[25]),
    ]
    order = (2, 0, 1)
    loads = {}
    for k in order:
        gradient = gd if k == 2 else ggu.at[:, pl.ds(k * FF, FF)]
        master = pout.at[0] if k == 2 else pin.at[k, 0]
        pairs = (
            (gradient, grads.at[k]),
            (master, masters.at[k]),
            (first.at[k, 0], firsts.at[k]),
            (second.at[k, 0], seconds.at[k]),
        )
        loads[k] = [
            pltpu.make_async_copy(src, dst, sem.at[k * 4 + i])
            for i, (src, dst) in enumerate(pairs)
        ]
        for copy in loads[k]:
            copy.start()
    for copy in passed:
        copy.start()
    stores = []
    for k in order:
        for copy in loads[k]:
            copy.wait()

        def tile(n, k=k):
            at = pl.ds(pl.multiple_of(n * 16, 16), 16)
            gradient = grads[k, at, :]
            master = masters[k, at, :]
            m = beta_one * firsts[k, at, :] + (1.0 - beta_one) * gradient
            v = beta_two * seconds[k, at, :] + (1.0 - beta_two) * gradient * gradient
            root = jnp.sqrt(v * (1.0 / bias_two)) + adam_eps
            step = (m * (1.0 / bias_one)) / root + decay_rate * master
            firsts[k, at, :] = m
            seconds[k, at, :] = v
            masters[k, at, :] = master - learn_rate * step

        loop(SH // 16, tile)
        new_master = new_out.at[0] if k == 2 else new_in.at[k, 0]
        pairs = (
            (masters.at[k], new_master),
            (firsts.at[k], new_first.at[k, 0]),
            (seconds.at[k], new_second.at[k, 0]),
        )
        for i, (src, dst) in enumerate(pairs):
            copy = pltpu.make_async_copy(src, dst, sem.at[12 + k * 4 + i])
            copy.start()
            stores.append(copy)
        if k == 2:
            for i, dst in enumerate((out_copy, tgrad_copy)):
                passed[i].wait()
                copy = pltpu.make_async_copy(held.at[i], dst, sem.at[26 + i])
                copy.start()
                stores.append(copy)
    for copy in stores:
        copy.wait()


def adam(ggu, gd, pin, pout, first, second, out, tgrad):
    hbm = pl.BlockSpec(memory_space=pl.ANY)
    arrays = (pin, pout, first, second, out, tgrad)
    return pl.pallas_call(
        adam_kernel,
        out_shape=[jax.ShapeDtypeStruct(a.shape, a.dtype) for a in arrays],
        in_specs=[hbm] * 8,
        out_specs=[hbm] * 6,
        scratch_shapes=[pltpu.VMEM((3, SH, FF), F32)] * 4
        + [pltpu.VMEM((2, TOK, D), BF), pltpu.SemaphoreType.DMA((28,))],
        compiler_params=pltpu.CompilerParams(vmem_limit_bytes=64 * 2**20),
        name="adam",
    )(ggu, gd, *arrays)


def per_device(
    tokens, route_ids, route_gates, out_grad, proj_in, proj_out, first_moment, second_moment
):
    layer_out, token_grad, ggu, gd = exchange(
        route_ids.T, route_gates.T, tokens, out_grad, proj_in, proj_out
    )
    new_in, new_out, new_first, new_second, layer_out, token_grad = adam(
        ggu, gd, proj_in, proj_out, first_moment, second_moment, layer_out, token_grad
    )
    return (layer_out, token_grad, new_in, new_out, new_first, new_second)


def solution(mesh):
    rows = P(("group", "member"), None)
    return jax.shard_map(
        per_device,
        mesh=mesh,
        in_specs=(
            rows,
            rows,
            rows,
            rows,
            P(None, "member", "group", None),
            P("member", "group", None),
            P(None, "member", "group", None),
            P(None, "member", "group", None),
        ),
        out_specs=(
            rows,
            rows,
            P(None, "member", "group", None),
            P("member", "group", None),
            P(None, "member", "group", None),
            P(None, "member", "group", None),
        ),
        check_vma=False,
    )
```

```python
import functools

import jax
import jax.numpy as jnp
from jax import lax
from jax.experimental import pallas as pl
from jax.experimental.pallas import tpu as pltpu
from jax.sharding import PartitionSpec as P

MESH = pl.DeviceIdType.MESH
BF = jnp.bfloat16
F32 = jnp.float32
CAP = 80
WIN = 4
TOK = 128
D = 2560
FF = 384
SH = 320
SLOTS = WIN * CAP
ROWS = 16 * CAP
HALF = 2 * CAP
CA = 1792
CC = 1536
CF = 1536
CG = 1792
SPLITS = (768, 1280)

beta_one = 0.9
beta_two = 0.95
learn_rate = 0.0003
decay_rate = 0.1
adam_eps = 1e-08
bias_one = 1.0 - 0.9**10
bias_two = 1.0 - 0.95**10

NN = (((1,), (0,)), ((), ()))
NT = (((1,), (1,)), ((), ()))
TN = (((0,), (0,)), ((), ()))


def dot(a, b, dims):
    return lax.dot_general(a, b, dims, preferred_element_type=F32)


def loop(count, body):
    lax.fori_loop(0, count, lambda i, c: (body(i), c)[1], 0)


def slot_table(z, ids_ref, gate_ref, table):
    ids = ids_ref[...]
    value = gate_ref[...].astype(F32)
    down = lax.broadcasted_iota(jnp.int32, (TOK, TOK), 0)
    lane = lax.broadcasted_iota(jnp.int32, (TOK, TOK), 1)
    row = lax.broadcasted_iota(jnp.int32, (8, TOK), 0)
    named = jnp.zeros((8, TOK), F32)
    match, weight = [], []
    for dz in range(WIN):
        hit = ids == (z - dz + WIN) % WIN
        match.append(jnp.sum(jnp.where(hit, 1.0, 0.0), axis=0, keepdims=True))
        weight.append(jnp.sum(jnp.where(hit, value, 0.0), axis=0, keepdims=True))
        named = jnp.where(row == dz, match[dz], named)
    upto = jnp.where(down <= lane, 1.0, 0.0).astype(BF)
    count = dot(named.astype(BF), upto, NN)
    for dz in range(WIN):
        table[dz : dz + 1, :] = jnp.where(match[dz] > 0, count[dz : dz + 1] - 1.0, -1.0)
        table[WIN + dz : WIN + dz + 1, :] = weight[dz]


def slot_gates(table, gates):
    slot = lax.broadcasted_iota(jnp.int32, (CAP, TOK), 0)
    for dz in range(WIN):
        place = table[dz : dz + 1, :].astype(jnp.int32)
        gate = jnp.where(slot == place, table[WIN + dz : WIN + dz + 1, :], 0.0)
        gates[pl.ds(dz * CAP, CAP), :] = gate.astype(BF)


def kernel(
    ids_ref,
    gate_ref,
    tok_hbm,
    cot_hbm,
    proj_in,
    proj_out,
    out_hbm,
    tgrad_hbm,
    ggu_hbm,
    gd_hbm,
    out_ref,
    tgrad_ref,
    ggu_ref,
    gd_ref,
    table,
    table_p,
    gates,
    gates_p,
    tok_p,
    cot_p,
    slots,
    slots_p,
    rows,
    cots,
    wgu,
    wd,
    hid,
    dgu,
    psend,
    pown,
    precv,
    ret,
    fin_recv0,
    fin_recv1,
    xret0,
    xret1,
    ggu,
    gd,
    y1gu,
    y1d,
    y2gu,
    y2d,
    xgu,
    xd,
    send_sem,
    recv_sem,
    loc_sem,
    credit,
):
    tok, cot, pre = out_ref, tgrad_ref, ggu_ref
    g = lax.axis_index("group")
    m = lax.axis_index("member")
    xh, y = g // 4, g % 4
    z, xc = m // 4, m % 4
    x, c = xc // 2, xc % 2
    to_core = (g, z * 4 + x * 2 + (1 - c))
    to_x = (g, z * 4 + (1 - x) * 2 + c)

    def at_z(step):
        return (g, ((z + step) % 4) * 4 + xc)

    y_up, y_dn, y_far = (y + 1) % 4, (y + 3) % 4, (y + 2) % 4
    to_yup = (xh * 4 + y_up, m)
    to_ydn = (xh * 4 + y_dn, m)
    to_xh = ((1 - xh) * 4 + y, m)

    used = [0, 0]
    free = []
    which = {}

    def send(src, dst, target):
        i = used[0]
        used[0] += 1
        if free:
            k = free.pop()
        else:
            k = used[1]
            used[1] += 1
        copy = pltpu.make_async_remote_copy(
            src_ref=src,
            dst_ref=dst,
            send_sem=send_sem.at[k],
            recv_sem=recv_sem.at[i],
            device_id=target,
            device_id_type=MESH,
        )
        copy.start()
        which[id(copy)] = k
        return copy

    loads = [
        pltpu.make_async_copy(tok_hbm, tok, loc_sem.at[8]),
        pltpu.make_async_copy(proj_in.at[0, 0], pre.at[:, pl.ds(0, FF)], loc_sem.at[9]),
        pltpu.make_async_copy(proj_in.at[1, 0], pre.at[:, pl.ds(FF, FF)], loc_sem.at[10]),
        pltpu.make_async_copy(proj_out.at[0], gd_ref, loc_sem.at[11]),
        pltpu.make_async_copy(cot_hbm, cot, loc_sem.at[12]),
    ]
    for copy in loads:
        copy.start()
    barrier = pltpu.get_barrier_semaphore()
    for other in (to_core, to_x, at_z(1), at_z(2), at_z(3), to_yup, to_ydn, to_xh):
        pl.semaphore_signal(barrier, inc=1, device_id=other, device_id_type=MESH)
    slot_table(z, ids_ref, gate_ref, table)
    slot_gates(table, gates)
    for copy in loads[:4]:
        copy.wait()
    own = pl.ds(pl.multiple_of((xh * 4 + y) * SH, SH), SH)
    wgu[own, :] = pre[...].astype(BF)
    wd[own, :] = gd_ref[...].astype(BF)
    pl.semaphore_wait(barrier, 8)

    def shard(ref, xh_, y_, first=0, count=SH):
        start = pl.multiple_of((xh_ * 4 + y_) * SH + first, 16)
        return ref.at[pl.ds(start, count)]

    def block(ref, dz, dc, dx):
        return ref.at[pl.ds(dz * SLOTS + dc * HALF + dx * CAP, CAP)]

    late = []

    c_gates = send(table, table_p, to_x)
    late.append(c_gates)

    def w_first(buf):
        part = shard(buf, xh, y)
        up = send(part, part, to_yup)
        dn = send(part, part, to_ydn)
        late.extend([up, dn])
        return up, dn

    def w_far(buf):
        far = send(shard(buf, xh, y), shard(buf, xh, y), to_xh)
        late.append(far)
        return far

    def w_second(buf, far):
        far.wait_recv()
        part = shard(buf, 1 - xh, y)
        up = send(part, part, to_yup)
        dn = send(part, part, to_ydn)
        late.extend([up, dn])
        return up, dn

    def w_forward(buf, xh_, pair):
        up, dn = pair
        up.wait_recv()
        part = shard(buf, xh_, y_dn, 0, SH // 2)
        on_up = send(part, part, to_yup)
        dn.wait_recv()
        part = shard(buf, xh_, y_up, SH // 2, SH // 2)
        on_dn = send(part, part, to_ydn)
        late.extend([on_up, on_dn])
        return on_up, on_dn

    gu0 = w_first(wgu)
    gu_far = w_far(wgu)

    def fill(mat_ref, val_ref, dst, dx, base, gated, width, step):
        held = (slots, slots_p)[dx]
        mat = mat_ref[...]
        if not gated:
            mat = jnp.where(mat > 0, jnp.ones_like(mat), jnp.zeros_like(mat))

        def tile(n):
            cols = pl.ds(pl.multiple_of(n * step, 128), step)
            val = dot(mat, val_ref[:, cols], NN).astype(BF)
            dst[pl.ds(dx * CAP, CAP), cols] = val[:CAP]
            held[pl.ds(base * 3 * CAP, 3 * CAP), cols] = val[CAP:]

        loop(width // step, tile)

    def x_first(dst):
        return pl.ds(0, CA if dst is rows else CC)

    def z_first(dst):
        return pl.ds(CA, D - CA) if dst is rows else pl.ds(CC, D - CC)

    def spread(dst, dx, base, dz):
        src = (slots, slots_p)[dx].at[pl.ds((base * 3 + dz - 1) * CAP, CAP)]
        land = block(dst, dz, 0, dx)
        if dx == 1:
            cols = x_first(dst)
            src, land = src.at[:, cols], land.at[:, cols]
        copy = send(src, land, at_z(4 - dz))
        late.append(copy)
        return copy

    def cross(dst, dz, dx, cols):
        copy = send(
            block(dst, dz, 0, dx).at[:, cols], block(dst, dz, 1, dx).at[:, cols], to_core
        )
        late.append(copy)
        return copy

    def own_in(dst, table, dz):
        table[dz, 0] = cross(dst, dz, 0, pl.ds(0, D))

    def own_on(dst, table, dz):
        cols = z_first(dst)
        copy = send(block(dst, dz, 0, 0).at[:, cols], block(dst, dz, 0, 1).at[:, cols], to_x)
        late.append(copy)
        table[dz, "x"] = copy

    def last_in(dst, table, dz):
        table[dz, "x"].wait_recv()
        table[dz, 2] = cross(dst, dz, 1, z_first(dst))

    core_tok, core_cot = {}, {}
    fill(gates, tok, rows, 0, 0, False, D, 512)
    z_tok0 = {dz: spread(rows, 0, 0, dz) for dz in (1, 3, 2)}
    own_in(rows, core_tok, 0)
    c_tok = send(tok.at[:, x_first(rows)], tok_p.at[:, x_first(rows)], to_x)
    loads[4].wait()
    fill(gates, cot, cots, 0, 1, True, D, 512)
    gu2 = w_forward(wgu, xh, gu0)
    gu1 = w_second(wgu, gu_far)
    for dz in (1, 3, 2):
        z_tok0[dz].wait_recv()
        own_in(rows, core_tok, dz)
    z_cot0 = {2: spread(cots, 0, 1, 2)}
    c_gates.wait_recv()
    slot_gates(table_p, gates_p)
    c_tok.wait_recv()
    for dz in (0, 1, 3, 2):
        own_on(rows, core_tok, dz)
    fill(gates_p, tok_p, rows, 1, 0, False, CA, CA // 2)
    z_tok1 = {dz: spread(rows, 1, 0, dz) for dz in (1, 3, 2)}
    core_tok[0, 1] = cross(rows, 0, 1, x_first(rows))
    d0 = w_first(wd)
    d_far = w_far(wd)
    gu3 = w_forward(wgu, 1 - xh, gu1)
    c_cot = send(cot.at[:, x_first(cots)], cot_p.at[:, x_first(cots)], to_x)
    z_cot0[1] = spread(cots, 0, 1, 1)
    z_cot0[3] = spread(cots, 0, 1, 3)
    d2 = w_forward(wd, xh, d0)
    d1 = w_second(wd, d_far)
    last_in(rows, core_tok, 0)
    own_in(cots, core_cot, 0)
    own_on(cots, core_cot, 0)
    for dz in (1, 3, 2):
        z_tok1[dz].wait_recv()
        core_tok[dz, 1] = cross(rows, dz, 1, x_first(rows))
    for dz in (1, 3, 2):
        last_in(rows, core_tok, dz)

    for copy in gu2 + gu3:
        copy.wait_recv()

    def forward_one(dz):
        here = pl.ds(dz * SLOTS, SLOTS)

        pre[...] = dot(rows[here, :], wgu[...], NN)

        def act(n):
            src = pl.ds(pl.multiple_of(n * 32, 32), 32)
            dst = pl.ds(pl.multiple_of(dz * SLOTS + n * 32, 32), 32)
            gate, up = pre[src, :FF], pre[src, FF:]
            sig = jax.nn.sigmoid(gate)
            active = gate * sig
            hid[dst, :] = (active * up).astype(BF)
            dgu[dst, :FF] = (up * (sig * (1.0 + gate * (1.0 - sig)))).astype(BF)
            dgu[dst, FF:] = active.astype(BF)

        loop(SLOTS // 32, act)

    def core_wait(table, dz):
        for part in range(3):
            table[dz, part].wait_recv()

    def cot_one(dz):
        z_cot0[dz].wait_recv()
        own_in(cots, core_cot, dz)
        own_on(cots, core_cot, dz)

    def cot_two(dz):
        z_cot1[dz].wait_recv()
        core_cot[dz, 1] = cross(cots, dz, 1, x_first(cots))
        last_in(cots, core_cot, dz)

    core_wait(core_tok, 0)
    forward_one(0)
    c_cot.wait_recv()
    fill(gates_p, cot_p, cots, 1, 1, True, CC, CC // 2)
    z_cot1 = {dz: spread(cots, 1, 1, dz) for dz in (1, 3, 2)}
    core_cot[0, 1] = cross(cots, 0, 1, x_first(cots))
    core_wait(core_tok, 1)
    forward_one(1)
    d3 = w_forward(wd, 1 - xh, d1)
    last_in(cots, core_cot, 0)
    core_wait(core_tok, 3)
    forward_one(3)
    for dz in (1, 3, 2):
        cot_one(dz)
    core_wait(core_tok, 2)
    forward_one(2)

    for copy in d2 + d3:
        copy.wait_recv()

    def product(left, right, dz, arr):
        here = pl.ds(dz * SLOTS, SLOTS)

        def tile(n):
            cols = pl.ds(pl.multiple_of(n * 1280, 256), 1280)
            val = dot(left[here, :], right[cols, :], NT).astype(BF)
            pown[pl.ds((arr * 4 + dz) * HALF, HALF), cols] = val[:HALF]
            psend[pl.ds(dz * HALF, HALF), cols] = val[HALF:]

        loop(D // 1280, tile)

    def hand_over(dz):
        part = pl.ds(dz * HALF, HALF)
        return send(psend.at[part], precv.at[part], to_core)

    def add_up(dz, arr, copy):
        copy.wait_recv()

        def tile(n):
            k = pl.multiple_of(n * 16, 16)
            a = pown[pl.ds((arr * 4 + dz) * HALF + k, 16), :].astype(F32)
            b = precv[pl.ds(dz * HALF + k, 16), :].astype(F32)
            pown[pl.ds((arr * 4 + dz) * HALF + k, 16), :] = (a + b).astype(BF)

        loop(HALF // 16, tile)

    parts = [
        (pl.ds(0, k), pl.ds(k, n - k), pl.ds(n, D - n)) for k, n in zip(SPLITS, (CF, CG))
    ]
    xrets = (xret0, xret1)

    def swap(dz, arr):
        src = pown.at[pl.ds((arr * 4 + dz) * HALF + CAP, CAP), parts[arr][2]]
        copy = send(src, xrets[arr].at[pl.ds(dz * CAP, CAP)], to_x)
        late.append(copy)
        swapped[arr, dz] = copy

    def add_swapped(dz, arr):
        swapped[arr, dz].wait_recv()
        cols = parts[arr][2]
        a = pown[pl.ds((arr * 4 + dz) * HALF, CAP), cols].astype(F32)
        b = xrets[arr][pl.ds(dz * CAP, CAP), :].astype(F32)
        pown[pl.ds((arr * 4 + dz) * HALF, CAP), cols] = (a + b).astype(BF)

    def give(dz, arr, n, dx):
        src = pown.at[pl.ds((arr * 4 + dz) * HALF + dx * CAP, CAP), parts[arr][n]]
        dst = ret.at[pl.ds((arr * 2 + dx) * SLOTS + dz * CAP, CAP), parts[arr][n]]
        if dz == 0:
            copy = pltpu.make_async_copy(src, dst, loc_sem.at[13 + arr * 5 + n * 2 + dx])
            copy.start()
        else:
            copy = send(src, dst, at_z(dz))
            late.append(copy)
        back[arr, n, dz, dx] = copy

    def give_back(arr, n):
        for dz in (1, 3, 2, 0):
            give(dz, arr, n, 0)
            give(dz, arr, n, 1)

    def give_last(arr):
        for dz in (1, 3, 2, 0):
            add_swapped(dz, arr)
            give(dz, arr, 2, 0)

    def given(arr, n):
        for dx in (0, 1) if n < 2 else (0,):
            back[arr, n, 0, dx].wait()
            for dz in (1, 3, 2):
                back[arr, n, dz, dx].wait_recv()

    order = (0, 1, 3, 2)
    hand, hand_b = {}, {}
    back, swapped = {}, {}
    for dz in order:
        product(hid, wd, dz, 0)
        hand[dz] = hand_over(dz)
    for dz in order:
        add_up(dz, 0, hand[dz])
        pl.semaphore_signal(credit.at[dz], inc=1, device_id=to_core, device_id_type=MESH)

    def backward_one(dz):
        here = pl.ds(dz * SLOTS, SLOTS)
        pre[:, :FF] = dot(cots[here, :], wd[...], NN)

        def act(n):
            src = pl.ds(pl.multiple_of(n * 32, 32), 32)
            dst = pl.ds(pl.multiple_of(dz * SLOTS + n * 32, 32), 32)
            dh = pre[src, :FF]
            dgu[dst, :FF] = (dgu[dst, :FF].astype(F32) * dh).astype(BF)
            dgu[dst, FF:] = (dgu[dst, FF:].astype(F32) * dh).astype(BF)

        loop(SLOTS // 32, act)

    def backward_two(dz):
        hand[dz].wait_send()
        pl.semaphore_wait(credit.at[dz], 1)
        product(dgu, wgu, dz, 1)
        hand_b[dz] = hand_over(dz)

    early = len(late)
    give_back(0, 0)
    cot_two(1)
    core_wait(core_cot, 0)
    backward_one(0)
    cot_two(3)
    backward_two(0)
    cot_two(2)
    for dz in (1, 3, 2):
        core_wait(core_cot, dz)
    give_back(0, 1)
    for dz in order:
        swap(dz, 0)

    near = y // 2
    other = 1 - xh

    def weight_grad(left, right, buf, xh_, pair):
        at = pl.ds(pl.multiple_of((xh_ * 2 + pair) * 2 * SH, 128), 2 * SH)
        buf[at, :] = dot(left[:, at], right[...], TN).astype(BF)

    def add_into(buf, start, land, k):
        def tile(n):
            r = pl.multiple_of(n * 16, 16)
            at = pl.ds(pl.multiple_of(start + r, 16), 16)
            a = buf[at, :].astype(F32) + land[k, pl.ds(r, 16), :].astype(F32)
            buf[at, :] = a.astype(BF)

        loop(SH // 2 // 16, tile)

    def ring_first(buf, land, k, xh_):
        up = send(shard(buf, xh_, y_far, 0, SH // 2), land.at[k], to_yup)
        dn = send(shard(buf, xh_, y_far, SH // 2, SH // 2), land.at[2 + k], to_ydn)
        late.extend([up, dn])
        return up, dn

    def ring_second(buf, land, land2, k, xh_, pair):
        up, dn = pair
        up.wait_recv()
        add_into(buf, (xh_ * 4 + y_up) * SH, land, k)
        on_up = send(shard(buf, xh_, y_up), land2.at[k], to_yup)
        dn.wait_recv()
        add_into(buf, (xh_ * 4 + y_dn) * SH + SH // 2, land, 2 + k)
        on_dn = send(shard(buf, xh_, y_dn), land2.at[2 + k], to_ydn)
        late.extend([on_up, on_dn])
        return on_up, on_dn

    def owner_value(buf, land, k, xh_):
        start = (xh_ * 4 + y) * SH

        def value(r):
            at = pl.ds(pl.multiple_of(start + r, 16), 16)
            here = pl.ds(r, 16)
            total = buf[at, :].astype(F32) + land[k, here, :].astype(F32)
            return total + land[2 + k, here, :].astype(F32)

        return start, value

    def ring_third(buf, land, recv, pair):
        for copy in pair:
            copy.wait_recv()
        start, value = owner_value(buf, land, 0, other)

        def tile(n):
            r = pl.multiple_of(n * 16, 16)
            buf[pl.ds(pl.multiple_of(start + r, 16), 16), :] = value(r).astype(BF)

        loop(SH // 16, tile)
        copy = send(shard(buf, other, y), recv, to_xh)
        late.append(copy)
        return copy

    def ring_last(buf, land, recv, out, pair, copy):
        for c_ in pair:
            c_.wait_recv()
        copy.wait_recv()
        _, value = owner_value(buf, land, 1, xh)

        def tile(n):
            r = pl.multiple_of(n * 16, 16)
            out[pl.ds(r, 16), :] = value(r) + recv[pl.ds(r, 16), :].astype(F32)

        loop(SH // 16, tile)

    def pick(mat_ref, arr):
        mat = mat_ref[...]
        return jnp.where(mat > 0, jnp.ones_like(mat), jnp.zeros_like(mat)) if arr else mat

    fins = {}
    fin_recv = (fin_recv0, fin_recv1)

    def combine(arr, n):
        given(arr, n)
        held = (cot_p, tok_p)[arr]
        part = ret[pl.ds((arr * 2 + 1) * SLOTS, SLOTS), parts[arr][n]]
        held[:, parts[arr][n]] = dot(pick(gates_p, arr), part, TN).astype(BF)
        copy = send(held.at[:, parts[arr][n]], fin_recv[arr].at[:, parts[arr][n]], to_x)
        late.append(copy)
        fins[arr, n] = copy

    def finish(arr, n, dst):
        if n == 2:
            given(arr, n)
        part = ret[pl.ds(arr * 2 * SLOTS, SLOTS), parts[arr][n]]
        total = dot(pick(gates, arr), part, TN)
        if n < 2:
            fins[arr, n].wait_recv()
            total = total + fin_recv[arr][:, parts[arr][n]].astype(F32)
        dst[:, parts[arr][n]] = total.astype(BF)

    def flush():
        for copy in late[:early]:
            copy.wait_send()
            free.append(which[id(copy)])
        del late[:early]

    def settle(dz):
        add_up(dz, 1, hand_b[dz])
        swap(dz, 1)

    weight_grad(cots, hid, gd, other, 1 - near)
    d_a = ring_first(gd, y1d, 0, other)
    weight_grad(cots, hid, gd, other, near)
    flush()
    for dz in (1, 3, 2):
        backward_one(dz)
    d_a = ring_second(gd, y1d, y2d, 0, other, d_a)
    weight_grad(rows, dgu, ggu, other, 1 - near)
    gu_a = ring_first(ggu, y1gu, 0, other)
    weight_grad(rows, dgu, ggu, other, near)
    settle(0)
    backward_two(1)
    backward_two(3)
    settle(1)
    backward_two(2)
    settle(3)
    gu_a = ring_second(ggu, y1gu, y2gu, 0, other, gu_a)
    give_last(0)
    settle(2)
    give_back(1, 0)
    weight_grad(cots, hid, gd, xh, 1 - near)
    d_b = ring_first(gd, y1d, 1, xh)
    weight_grad(cots, hid, gd, xh, near)
    weight_grad(rows, dgu, ggu, xh, 1 - near)
    c_tok.wait_send()
    c_cot.wait_send()
    combine(0, 0)
    combine(0, 1)
    gu_b = ring_first(ggu, y1gu, 1, xh)
    d_x = ring_third(gd, y2d, xd, d_a)
    weight_grad(rows, dgu, ggu, xh, near)
    give_back(1, 1)
    gu_x = ring_third(ggu, y2gu, xgu, gu_a)
    d_b = ring_second(gd, y1d, y2d, 1, xh, d_b)
    gu_b = ring_second(ggu, y1gu, y2gu, 1, xh, gu_b)
    give_last(1)
    finish(0, 2, out_ref)
    stores = []

    def store(src, dst):
        copy = pltpu.make_async_copy(src, dst, loc_sem.at[23 + len(stores)])
        copy.start()
        stores.append(copy)

    ring_last(gd, y2d, xd, gd_ref, d_b, d_x)
    store(gd_ref, gd_hbm)
    finish(0, 0, out_ref)
    finish(0, 1, out_ref)
    store(out_ref, out_hbm)
    combine(1, 0)
    combine(1, 1)
    finish(1, 0, tgrad_ref)
    store(tgrad_ref.at[:, parts[1][0]], tgrad_hbm.at[:, parts[1][0]])
    ring_last(ggu, y2gu, xgu, ggu_ref, gu_b, gu_x)
    store(ggu_ref, ggu_hbm)
    finish(1, 2, tgrad_ref)
    store(tgrad_ref.at[:, parts[1][2]], tgrad_hbm.at[:, parts[1][2]])
    finish(1, 1, tgrad_ref)
    store(tgrad_ref.at[:, parts[1][1]], tgrad_hbm.at[:, parts[1][1]])
    for copy in stores:
        copy.wait()

    for copy in late:
        copy.wait_send()
    for dz in order:
        hand_b[dz].wait_send()
    assert used == [N_COPY, N_SEND], used


N_COPY, N_SEND = 133, 88


def exchange(ids, gates, tok, cot, proj_in, proj_out):
    vmem = pl.BlockSpec(memory_space=pltpu.VMEM)
    hbm = pl.BlockSpec(memory_space=pl.ANY)
    shapes = [
        jax.ShapeDtypeStruct((TOK, D), BF),
        jax.ShapeDtypeStruct((TOK, D), BF),
        jax.ShapeDtypeStruct((SH, 2 * FF), F32),
        jax.ShapeDtypeStruct((SH, FF), F32),
    ]
    scratch = [
        pltpu.VMEM((TOK, D), BF),
        pltpu.VMEM((TOK, D), BF),
        pltpu.VMEM((SH, 2 * FF), F32),
        pltpu.VMEM((SH, FF), F32),
        pltpu.VMEM((2 * WIN, TOK), F32),
        pltpu.VMEM((2 * WIN, TOK), F32),
        pltpu.VMEM((SLOTS, TOK), BF),
        pltpu.VMEM((SLOTS, TOK), BF),
        pltpu.VMEM((TOK, max(CA, CG)), BF),
        pltpu.VMEM((TOK, max(CC, CF)), BF),
        pltpu.VMEM((6 * CAP, D), BF),
        pltpu.VMEM((6 * CAP, CA), BF),
        pltpu.VMEM((ROWS, D), BF),
        pltpu.VMEM((ROWS, D), BF),
        pltpu.VMEM((D, 2 * FF), BF),
        pltpu.VMEM((D, FF), BF),
        pltpu.VMEM((ROWS, FF), BF),
        pltpu.VMEM((ROWS, 2 * FF), BF),
        pltpu.VMEM((4 * HALF, D), BF),
        pltpu.VMEM((8 * HALF, D), BF),
        pltpu.VMEM((4 * HALF, D), BF),
        pltpu.VMEM((4 * SLOTS, D), BF),
        pltpu.VMEM((TOK, CF), BF),
        pltpu.VMEM((TOK, CG), BF),
        pltpu.VMEM((SLOTS, D - CF), BF),
        pltpu.VMEM((SLOTS, D - CG), BF),
        pltpu.VMEM((D, 2 * FF), BF),
        pltpu.VMEM((D, FF), BF),
        pltpu.VMEM((4, SH // 2, 2 * FF), BF),
        pltpu.VMEM((4, SH // 2, FF), BF),
        pltpu.VMEM((4, SH, 2 * FF), BF),
        pltpu.VMEM((4, SH, FF), BF),
        pltpu.VMEM((SH, 2 * FF), BF),
        pltpu.VMEM((SH, FF), BF),
        pltpu.SemaphoreType.DMA((N_SEND,)),
        pltpu.SemaphoreType.DMA((N_COPY,)),
        pltpu.SemaphoreType.DMA((29,)),
        pltpu.SemaphoreType.REGULAR((4,)),
    ]
    return pl.pallas_call(
        kernel,
        out_shape=shapes,
        in_specs=[vmem] * 2 + [hbm] * 4,
        out_specs=[hbm] * 4,
        scratch_shapes=scratch,
        compiler_params=pltpu.CompilerParams(
            collective_id=0, has_side_effects=True, vmem_limit_bytes=64 * 2**20
        ),
        cost_estimate=pl.CostEstimate(
            flops=18 * ROWS * D * FF, bytes_accessed=2**22, transcendentals=ROWS * FF
        ),
        name="experts",
    )(ids, gates, tok, cot, proj_in, proj_out)


def adam_kernel(*refs):
    ggu, gd, pin, pout, first, second, out, tgrad = refs[:8]
    new_in, new_out, new_first, new_second, out_copy, tgrad_copy = refs[8:14]
    grads, masters, firsts, seconds, held, sem = refs[14:]
    passed = [
        pltpu.make_async_copy(out, held.at[0], sem.at[24]),
        pltpu.make_async_copy(tgrad, held.at[1], sem.at[25]),
    ]
    order = (2, 0, 1)
    loads = {}
    for k in order:
        gradient = gd if k == 2 else ggu.at[:, pl.ds(k * FF, FF)]
        master = pout.at[0] if k == 2 else pin.at[k, 0]
        pairs = (
            (gradient, grads.at[k]),
            (master, masters.at[k]),
            (first.at[k, 0], firsts.at[k]),
            (second.at[k, 0], seconds.at[k]),
        )
        loads[k] = [
            pltpu.make_async_copy(src, dst, sem.at[k * 4 + i])
            for i, (src, dst) in enumerate(pairs)
        ]
        for copy in loads[k]:
            copy.start()
    for copy in passed:
        copy.start()
    stores = []
    for k in order:
        for copy in loads[k]:
            copy.wait()

        def tile(n, k=k):
            at = pl.ds(pl.multiple_of(n * 80, 16), 80)
            gradient = grads[k, at, :]
            master = masters[k, at, :]
            m = beta_one * firsts[k, at, :] + (1.0 - beta_one) * gradient
            v = beta_two * seconds[k, at, :] + (1.0 - beta_two) * gradient * gradient
            root = jnp.sqrt(v * (1.0 / bias_two)) + adam_eps
            step = (m * (1.0 / bias_one)) / root + decay_rate * master
            firsts[k, at, :] = m
            seconds[k, at, :] = v
            masters[k, at, :] = master - learn_rate * step

        loop(SH // 80, tile)
        new_master = new_out.at[0] if k == 2 else new_in.at[k, 0]
        pairs = (
            (masters.at[k], new_master),
            (firsts.at[k], new_first.at[k, 0]),
            (seconds.at[k], new_second.at[k, 0]),
        )
        for i, (src, dst) in enumerate(pairs):
            copy = pltpu.make_async_copy(src, dst, sem.at[12 + k * 4 + i])
            copy.start()
            stores.append(copy)
        if k == 2:
            for i, dst in enumerate((out_copy, tgrad_copy)):
                passed[i].wait()
                copy = pltpu.make_async_copy(held.at[i], dst, sem.at[26 + i])
                copy.start()
                stores.append(copy)
    for copy in stores:
        copy.wait()


def adam(ggu, gd, pin, pout, first, second, out, tgrad):
    hbm = pl.BlockSpec(memory_space=pl.ANY)
    arrays = (pin, pout, first, second, out, tgrad)
    return pl.pallas_call(
        adam_kernel,
        out_shape=[jax.ShapeDtypeStruct(a.shape, a.dtype) for a in arrays],
        in_specs=[hbm] * 8,
        out_specs=[hbm] * 6,
        scratch_shapes=[pltpu.VMEM((3, SH, FF), F32)] * 4
        + [pltpu.VMEM((2, TOK, D), BF), pltpu.SemaphoreType.DMA((28,))],
        compiler_params=pltpu.CompilerParams(vmem_limit_bytes=64 * 2**20),
        name="adam",
    )(ggu, gd, *arrays)


def per_device(
    tokens, route_ids, route_gates, out_grad, proj_in, proj_out, first_moment, second_moment
):
    layer_out, token_grad, ggu, gd = exchange(
        route_ids.T, route_gates.T, tokens, out_grad, proj_in, proj_out
    )
    new_in, new_out, new_first, new_second, layer_out, token_grad = adam(
        ggu, gd, proj_in, proj_out, first_moment, second_moment, layer_out, token_grad
    )
    return (layer_out, token_grad, new_in, new_out, new_first, new_second)


def solution(mesh):
    rows = P(("group", "member"), None)
    return jax.shard_map(
        per_device,
        mesh=mesh,
        in_specs=(
            rows,
            rows,
            rows,
            rows,
            P(None, "member", "group", None),
            P("member", "group", None),
            P(None, "member", "group", None),
            P(None, "member", "group", None),
        ),
        out_specs=(
            rows,
            rows,
            P(None, "member", "group", None),
            P("member", "group", None),
            P(None, "member", "group", None),
            P(None, "member", "group", None),
        ),
        check_vma=False,
    )
```
